512 devices in a mesh: dp: 16 (over z), seq: 32 (over y, x, core).
Axes of the slice: x: 4, y: 4, z: 16, core: 2. Of those that a mesh axis runs over, the one named last changes fastest.
Arguments:
- inputs: bfloat16 [16, 128, 4096], P('dp', None, 'seq'), may hold values from -6 to 6
- gate_values: bfloat16 [16, 128, 4096], P('dp', None, 'seq'), may hold values from -6 to 6
- grad_out: bfloat16 [16, 128, 4096], P('dp', None, 'seq'), may hold values from -6 to 6
- filter_raw: bfloat16 [128, 4096], P(None, 'seq'), may hold values from -6 to 6
- skip_gain: float32 [128], replicated, may hold values from 0.5 to 2
Outputs:
- d_input: bfloat16 [16, 128, 4096], P('dp', None, 'seq')
- d_gate: bfloat16 [16, 128, 4096], P('dp', None, 'seq')
- d_filter: float32 [128, 4096], P(None, 'seq')
The draws below stay inside these ranges and needn't reach their ends.
All inputs are finite; a program needn't handle non-finite values.
Results may differ from the reference program's by a relative error of at most 0.001.
Values may be sent and summed in bfloat16 or wider, within the bound.
No kernel may reach another device: no remote copies, remote signals or barrier semaphores. Data moves between devices by JAX's collectives and lax.ppermute only.
A program may use at most 64 MiB of HBM per device.

```python
import math
import jax
import jax.numpy as jnp
from jax import lax

CH = 128
SEQ_LEN = 4096
SEQS = 16


def block_scale(rng, shape, pieces, smallest, high):
    level = 1.0
    for position, parts in pieces:
        draws = jax.random.uniform(jax.random.fold_in(jax.random.fold_in(rng, 6), position), (parts,), jnp.float32, smallest / len(pieces), high / len(pieces))
        level = level * jnp.repeat(jnp.exp(draws), shape[position] // parts).reshape((-1,) + (1,) * (len(shape) - 1 - position))
    return level


def normal_values(key, dims, spread, limit, cuts=(), dtype=jnp.bfloat16):
    values = spread * jax.random.normal(key, dims, jnp.float32)
    if cuts:
        values = values * block_scale(key, dims, cuts, -0.22, 0.18)
    return jnp.clip(values, -limit, limit).astype(dtype)


def setup_inputs(seed: int = 0) -> dict:
    key_of = jax.random.split(jax.random.key(seed), 6)
    return {
        "inputs": normal_values(key_of[0], (SEQS, CH, SEQ_LEN), 1.0, 6.0, ((0, 16), (2, 32))),
        "gate_values": normal_values(key_of[1], (SEQS, CH, SEQ_LEN), 1.0, 6.0, ((0, 16), (2, 32))),
        "grad_out": normal_values(key_of[2], (SEQS, CH, SEQ_LEN), 1.0, 6.0, ((0, 16), (2, 32))),
        "filter_raw": normal_values(key_of[3], (CH, SEQ_LEN), 1.0, 6.0, ((1, 32),)),
        "skip_gain": jnp.clip(jnp.exp(jax.random.uniform(key_of[4], (CH,), jnp.float32, math.log(0.5), math.log(2.0))), 0.5, 2.0),
    }


def reference(inputs, gate_values, grad_out, filter_raw, skip_gain):
    seq_len = inputs.shape[-1]
    total = 2 * seq_len
    signal = inputs.astype(jnp.float32)
    gate_f = gate_values.astype(jnp.float32)
    grad_f = grad_out.astype(jnp.float32)
    kernel = filter_raw.astype(jnp.float32) / math.sqrt(seq_len)
    grad_conv = grad_f * gate_f
    kernel_hat = jnp.fft.rfft(kernel, n=total)
    signal_hat = jnp.fft.rfft(signal, n=total)
    grad_hat = jnp.fft.rfft(grad_conv, n=total)
    conv = jnp.fft.irfft(signal_hat * kernel_hat[None], n=total)[..., :seq_len]
    corr = jnp.fft.irfft(grad_hat * jnp.conj(kernel_hat)[None], n=total)[..., :seq_len]
    filt = jnp.fft.irfft(grad_hat * jnp.conj(signal_hat), n=total)[..., :seq_len]
    gains = skip_gain[None, :, None]
    d_gate = (grad_f * (conv + gains * signal)).astype(jnp.bfloat16)
    d_input = (corr + gains * grad_conv).astype(jnp.bfloat16)
    d_filter = lax.optimization_barrier(jnp.sum(filt, axis=0)) / math.sqrt(seq_len)
    return (d_input, d_gate, d_filter)
```

```python
import jax
import jax.numpy as jnp
from jax import lax
from jax.experimental import pallas as pl
from jax.experimental.pallas import tpu as pltpu
from jax.sharding import Mesh, PartitionSpec as P

LANES = 128
GROUP = 4
ROLES = 4

F32 = jnp.float32
BF16 = jnp.bfloat16


def iota(shape, dim):
    return lax.broadcasted_iota(jnp.int32, shape, dim)


def pack_kernel(u_ref, g_ref, y_ref, k_ref, out_ref, rows):
    chans = u_ref.shape[0]
    for role, ref in enumerate((u_ref, g_ref, y_ref, k_ref)):
        rows[pl.ds(role, chans, stride=ROLES), :] = ref[...].astype(F32)
    out_ref[...] = rows[...].astype(BF16)


def flip_rows(count, span):
    row, col = iota((count, count), 0), iota((count, count), 1)
    same = row // span == col // span
    return jnp.where(same & (row % span + col % span == span - 1), 1.0, 0.0).astype(BF16)


def conv_kernel(blocks, chan_ref, gain_ref, in_ref, gate_ref, input_ref, filt_ref, rows, padded, filt_rows):
    count = GROUP * blocks
    rows[...] = in_ref[...].astype(F32)
    u = rows[pl.ds(0, count, stride=ROLES), :]
    g = rows[pl.ds(1, count, stride=ROLES), :]
    y = rows[pl.ds(2, count, stride=ROLES), :]
    k = rows[pl.ds(3, blocks, stride=ROLES), :]
    gc = g * y
    high = gc.astype(BF16)
    low = (gc - high.astype(F32)).astype(BF16)

    lane_flip = flip_rows(LANES, LANES)
    flip = flip_rows(2 * count, blocks)
    both = jnp.concatenate([high, low], axis=0)
    both = jnp.dot(both, lane_flip, preferred_element_type=F32).astype(BF16)
    both = jnp.dot(flip, both, preferred_element_type=F32)
    turned_u = jnp.dot(flip[:count, :count], u.astype(BF16), preferred_element_type=F32)
    left = jnp.transpose(turned_u).astype(BF16)
    left = jnp.concatenate([left, left], axis=1)

    for part in range(3 * GROUP):
        padded[part, :blocks, :] = jnp.zeros((blocks, LANES), F32)
        if part < GROUP:
            value = u[part * blocks : (part + 1) * blocks]
        else:
            at = (part - GROUP) * blocks
            value = both[at : at + blocks]
        padded[part, blocks:, :] = value

    row, col = iota((LANES, LANES), 0), iota((LANES, LANES), 1)
    inside = col >= row
    zero = jnp.zeros((LANES, LANES), F32)
    before = zero
    total = jnp.zeros((3 * count, LANES), F32)
    held = None
    for pair in range(blocks // 2):
        shifted, toeplitz = [], []
        for d in (2 * pair, 2 * pair + 1):
            shifted.append(
                jnp.concatenate([padded[part, blocks - d : 2 * blocks - d, :] for part in range(3 * GROUP)], axis=0).astype(BF16)
            )
            spread = jnp.broadcast_to(k[d : d + 1, :], (LANES, LANES))
            rolled = pltpu.roll(spread, 0, 1, stride=1, stride_axis=0)
            toeplitz.append(jnp.where(inside, rolled, before).astype(BF16))
            before = rolled
        wide = jnp.concatenate(shifted, axis=1)
        total = total + jnp.dot(wide, jnp.concatenate(toeplitz, axis=0), preferred_element_type=F32)
        products = jnp.dot(left, wide[count:], preferred_element_type=F32)
        for half in range(2):
            d = 2 * pair + half
            turned = pltpu.roll(products[:, half * LANES : (half + 1) * LANES], 0, 1, stride=1, stride_axis=0)
            if held is not None:
                filt_rows[d - 1 : d, :] = jnp.sum(jnp.where(inside, held, turned), axis=0, keepdims=True)
            held = turned
    filt_rows[blocks - 1 : blocks, :] = jnp.sum(jnp.where(inside, held, 0.0), axis=0, keepdims=True)

    scale = 1.0 / 64.0
    gain = gain_ref[chan_ref[0]]
    gate_ref[...] = (y * (total[:count] * scale + gain * u)).astype(BF16)
    corr = total[count : 2 * count] + total[2 * count :]
    turned_gc = both[:count] + both[count:]
    d_input = (corr * scale + gain * turned_gc).astype(BF16)
    d_input = jnp.dot(d_input, lane_flip, preferred_element_type=F32).astype(BF16)
    input_ref[...] = jnp.dot(flip[:count, :count], d_input, preferred_element_type=F32).astype(BF16)
    filt = jnp.dot(filt_rows[...], lane_flip.astype(F32), precision=lax.Precision.HIGHEST, preferred_element_type=F32)
    for copy in range(filt_ref.shape[0]):
        filt_ref[copy] = filt


def spread_kernel(blocks, gate_ref, input_ref, filt_ref, out_ref, rows):
    count = GROUP * blocks
    filt = filt_ref[0]
    for copy in range(1, filt_ref.shape[0]):
        filt = filt + filt_ref[copy]
    high = filt.astype(BF16).astype(F32)
    low = filt - high
    rows[pl.ds(0, count, stride=ROLES), :] = gate_ref[...].astype(F32)
    rows[pl.ds(1, count, stride=ROLES), :] = input_ref[...].astype(F32)
    for part in range(GROUP):
        at = part * blocks * ROLES
        rows[pl.ds(at + 2, blocks, stride=ROLES), :] = high
        rows[pl.ds(at + 3, blocks, stride=ROLES), :] = low
    out_ref[...] = rows[...].astype(BF16)


def unpack_kernel(in_ref, input_ref, gate_ref, filt_ref, rows):
    chans = input_ref.shape[0]
    rows[...] = in_ref[...].astype(F32)
    gate_ref[...] = rows[pl.ds(0, chans, stride=ROLES), :].astype(BF16)
    input_ref[...] = rows[pl.ds(1, chans, stride=ROLES), :].astype(BF16)
    filt = rows[pl.ds(2, chans, stride=ROLES), :] + rows[pl.ds(3, chans, stride=ROLES), :]
    filt_ref[...] = filt * (1.0 / 64.0)


VMEM = pl.BlockSpec(memory_space=pltpu.VMEM)
SMEM = pl.BlockSpec(memory_space=pltpu.SMEM)


def shape(dims, dtype):
    return jax.ShapeDtypeStruct(dims, dtype)


def body(inputs, gate_values, grad_out, filter_raw, skip_gain):
    blocks = lax.axis_size("seq")
    far = lax.axis_size("far")
    chans = inputs.shape[1]
    count = GROUP * blocks
    params = pltpu.CompilerParams(vmem_limit_bytes=48 * 1024 * 1024)
    packed = pl.pallas_call(
        pack_kernel,
        out_shape=shape((chans * ROLES, LANES), BF16),
        in_specs=[VMEM] * 4,
        out_specs=VMEM,
        scratch_shapes=[pltpu.VMEM((chans * ROLES, LANES), F32)],
        compiler_params=params,
    )(inputs[0], gate_values[0], grad_out[0], filter_raw)
    packed = lax.all_to_all(packed, ("near", "seq"), 0, 0, tiled=True)
    chan = (lax.axis_index("near") * blocks + lax.axis_index("seq")).reshape(1)
    gate, d_in, filt = pl.pallas_call(
        lambda *refs: conv_kernel(blocks, *refs),
        out_shape=(shape((count, LANES), BF16), shape((count, LANES), BF16), shape((far, blocks, LANES), F32)),
        in_specs=[SMEM, SMEM, VMEM],
        out_specs=(VMEM, VMEM, VMEM),
        scratch_shapes=[
            pltpu.VMEM((count * ROLES, LANES), F32),
            pltpu.VMEM((3 * GROUP, 2 * blocks, LANES), F32),
            pltpu.VMEM((blocks, LANES), F32),
        ],
        compiler_params=params,
    )(chan, skip_gain, packed)
    filt = lax.all_to_all(filt, "far", 0, 0, tiled=True)
    packed = pl.pallas_call(
        lambda *refs: spread_kernel(blocks, *refs),
        out_shape=shape((count * ROLES, LANES), BF16),
        in_specs=[VMEM] * 3,
        out_specs=VMEM,
        scratch_shapes=[pltpu.VMEM((count * ROLES, LANES), F32)],
        compiler_params=params,
    )(gate, d_in, filt)
    packed = lax.all_to_all(packed, ("near", "seq"), 0, 0, tiled=True)
    d_input, d_gate, d_filter = pl.pallas_call(
        unpack_kernel,
        out_shape=(shape((chans, LANES), BF16), shape((chans, LANES), BF16), shape((chans, LANES), F32)),
        in_specs=[VMEM],
        out_specs=(VMEM, VMEM, VMEM),
        scratch_shapes=[pltpu.VMEM((chans * ROLES, LANES), F32)],
        compiler_params=params,
    )(packed)
    return d_input[None], d_gate[None], d_filter


def solution(mesh):
    sizes = mesh.devices.shape
    mesh = Mesh(mesh.devices.reshape(sizes[0] // GROUP, GROUP, sizes[1]), ("far", "near", "seq"))
    signal = P(("far", "near"), None, "seq")
    return jax.shard_map(
        body,
        mesh=mesh,
        in_specs=(signal, signal, signal, P(None, "seq"), P()),
        out_specs=(signal, signal, P(None, "seq")),
        check_vma=False,
    )
```

```python
import jax
import jax.numpy as jnp
from jax import lax
from jax.experimental import pallas as pl
from jax.experimental.pallas import tpu as pltpu
from jax.sharding import Mesh, PartitionSpec as P

LANES = 128
GROUP = 4
ROLES = 4

F32 = jnp.float32
BF16 = jnp.bfloat16


def iota(shape, dim):
    return lax.broadcasted_iota(jnp.int32, shape, dim)


def pack_kernel(u_ref, g_ref, y_ref, k_ref, out_ref, landed, rows, sems):
    chans = out_ref.shape[0] // ROLES
    copies = [
        pltpu.make_async_copy(ref, landed.at[role], sems.at[role])
        for role, ref in enumerate((u_ref, g_ref, y_ref, k_ref))
    ]
    for copy in copies:
        copy.start()
    for role, copy in enumerate(copies):
        copy.wait()
        rows[pl.ds(role, chans, stride=ROLES), :] = landed[role].astype(F32)
    out_ref[...] = rows[...].astype(BF16)


def flip_rows(count, span):
    row, col = iota((count, count), 0), iota((count, count), 1)
    same = row // span == col // span
    return jnp.where(same & (row % span + col % span == span - 1), 1.0, 0.0).astype(BF16)


def take(rows, role, count):
    return rows[pl.ds(role, count, stride=ROLES), :]


def flipped_pair(gc, flip, lane_flip):
    high = gc.astype(BF16)
    low = (gc - high.astype(F32)).astype(BF16)
    both = jnp.concatenate([high, low], axis=0)
    both = jnp.dot(both, lane_flip, preferred_element_type=F32).astype(BF16)
    return jnp.dot(flip, both, preferred_element_type=F32)


def pad(padded, value, blocks):
    for part in range(padded.shape[0]):
        padded[part, :blocks, :] = jnp.zeros((blocks, LANES), F32)
        padded[part, blocks:, :] = value[part * blocks : (part + 1) * blocks]


def shifted(padded, d, blocks):
    parts = [padded[part, blocks - d : 2 * blocks - d, :] for part in range(padded.shape[0])]
    return jnp.concatenate(parts, axis=0).astype(BF16)


def skew(value):
    return pltpu.roll(value, 0, 1, stride=1, stride_axis=0)


def filt_kernel(blocks, in_ref, filt_ref, rows, padded, filt_rows):
    count = GROUP * blocks
    rows[...] = in_ref[...].astype(F32)
    u = take(rows, 0, count)
    gc = take(rows, 1, count) * take(rows, 2, count)
    lane_flip = flip_rows(LANES, LANES)
    flip = flip_rows(2 * count, blocks)
    pad(padded, flipped_pair(gc, flip, lane_flip), blocks)
    turned_u = jnp.dot(flip[:count, :count], u.astype(BF16), preferred_element_type=F32)
    left = jnp.transpose(turned_u).astype(BF16)
    left = jnp.concatenate([left, left], axis=1)
    inside = iota((LANES, LANES), 1) >= iota((LANES, LANES), 0)
    held = None
    for pair in range(blocks // 2):
        wide = jnp.concatenate([shifted(padded, 2 * pair, blocks), shifted(padded, 2 * pair + 1, blocks)], axis=1)
        products = jnp.dot(left, wide, preferred_element_type=F32)
        for half in range(2):
            d = 2 * pair + half
            turned = skew(products[:, half * LANES : (half + 1) * LANES])
            if held is not None:
                filt_rows[d - 1 : d, :] = jnp.sum(jnp.where(inside, held, turned), axis=0, keepdims=True)
            held = turned
    filt_rows[blocks - 1 : blocks, :] = jnp.sum(jnp.where(inside, held, 0.0), axis=0, keepdims=True)
    filt_ref[...] = jnp.dot(
        filt_rows[...], lane_flip.astype(F32), precision=lax.Precision.HIGHEST, preferred_element_type=F32
    )


def conv_kernel(blocks, chan_ref, gain_ref, in_ref, gate_ref, input_ref, rows, padded, gains, sem):
    count = GROUP * blocks
    fetch = pltpu.make_async_copy(gain_ref, gains, sem)
    fetch.start()
    rows[...] = in_ref[...].astype(F32)
    u = take(rows, 0, count)
    y = take(rows, 2, count)
    gc = take(rows, 1, count) * y
    k = take(rows, 3, blocks)
    lane_flip = flip_rows(LANES, LANES)
    flip = flip_rows(2 * count, blocks)
    both = flipped_pair(gc, flip, lane_flip)
    pad(padded, jnp.concatenate([u, both], axis=0), blocks)
    inside = iota((LANES, LANES), 1) >= iota((LANES, LANES), 0)
    before = jnp.zeros((LANES, LANES), F32)
    total = jnp.zeros((3 * count, LANES), F32)
    for pair in range(blocks // 2):
        signal, toeplitz = [], []
        for d in (2 * pair, 2 * pair + 1):
            signal.append(shifted(padded, d, blocks))
            rolled = skew(jnp.broadcast_to(k[d : d + 1, :], (LANES, LANES)))
            toeplitz.append(jnp.where(inside, rolled, before).astype(BF16))
            before = rolled
        total = total + jnp.dot(
            jnp.concatenate(signal, axis=1), jnp.concatenate(toeplitz, axis=0), preferred_element_type=F32
        )
    scale = 1.0 / 64.0
    fetch.wait()
    gain = gains[chan_ref[0]]
    gate_ref[...] = (y * (total[:count] * scale + gain * u)).astype(BF16)
    corr = total[count : 2 * count] + total[2 * count :]
    d_input = (corr * scale + gain * (both[:count] + both[count:])).astype(BF16)
    d_input = jnp.dot(d_input, lane_flip, preferred_element_type=F32).astype(BF16)
    input_ref[...] = jnp.dot(flip[:count, :count], d_input, preferred_element_type=F32).astype(BF16)


def spread_kernel(blocks, gate_ref, input_ref, near_ref, far_ref, out_ref, rows):
    count = GROUP * blocks
    filt = near_ref[...] + far_ref[...]
    high = filt.astype(BF16).astype(F32)
    low = filt - high
    rows[pl.ds(0, count, stride=ROLES), :] = gate_ref[...].astype(F32)
    rows[pl.ds(1, count, stride=ROLES), :] = input_ref[...].astype(F32)
    for part in range(GROUP):
        at = part * blocks * ROLES
        rows[pl.ds(at + 2, blocks, stride=ROLES), :] = high
        rows[pl.ds(at + 3, blocks, stride=ROLES), :] = low
    out_ref[...] = rows[...].astype(BF16)


def unpack_kernel(in_ref, input_ref, gate_ref, filt_ref, rows):
    chans = input_ref.shape[0]
    rows[...] = in_ref[...].astype(F32)
    gate_ref[...] = take(rows, 0, chans).astype(BF16)
    input_ref[...] = take(rows, 1, chans).astype(BF16)
    filt_ref[...] = (take(rows, 2, chans) + take(rows, 3, chans)) * (1.0 / 64.0)


VMEM = pl.BlockSpec(memory_space=pltpu.VMEM)
SMEM = pl.BlockSpec(memory_space=pltpu.SMEM)


def shape(dims, dtype):
    return jax.ShapeDtypeStruct(dims, dtype)


HBM = pl.BlockSpec(memory_space=pltpu.HBM)


def call(kernel, outs, ins, scratch, limit=48):
    return pl.pallas_call(
        kernel,
        out_shape=outs,
        in_specs=ins,
        out_specs=jax.tree.map(lambda _: VMEM, outs),
        scratch_shapes=scratch,
        compiler_params=pltpu.CompilerParams(vmem_limit_bytes=limit * 1024 * 1024),
    )


def body(inputs, gate_values, grad_out, filter_raw, skip_gain):
    blocks = lax.axis_size("seq")
    far = lax.axis_size("far")
    chans = inputs.shape[1]
    count = GROUP * blocks
    rows = pltpu.VMEM((count * ROLES, LANES), F32)
    packed = call(
        pack_kernel,
        shape((chans * ROLES, LANES), BF16),
        [HBM] * 4,
        [
            pltpu.VMEM((ROLES, chans, LANES), BF16),
            pltpu.VMEM((chans * ROLES, LANES), F32),
            pltpu.SemaphoreType.DMA((ROLES,)),
        ],
        60,
    )(inputs[0], gate_values[0], grad_out[0], filter_raw)
    packed = lax.all_to_all(packed, ("near", "seq"), 0, 0, tiled=True)
    filt = call(
        lambda *refs: filt_kernel(blocks, *refs),
        shape((blocks, LANES), F32),
        [VMEM],
        [rows, pltpu.VMEM((2 * GROUP, 2 * blocks, LANES), F32), pltpu.VMEM((blocks, LANES), F32)],
    )(packed)
    opposite = lax.ppermute(filt, "far", [(i, i ^ 2) for i in range(far)])
    chan = (lax.axis_index("near") * blocks + lax.axis_index("seq")).reshape(1)
    gate, d_in = call(
        lambda *refs: conv_kernel(blocks, *refs),
        (shape((count, LANES), BF16), shape((count, LANES), BF16)),
        [SMEM, HBM, VMEM],
        [
            rows,
            pltpu.VMEM((3 * GROUP, 2 * blocks, LANES), F32),
            pltpu.SMEM(skip_gain.shape, F32),
            pltpu.SemaphoreType.DMA(()),
        ],
    )(chan, skip_gain, packed)
    filt = filt + opposite
    beside = lax.ppermute(filt, "far", [(i, i ^ 1) for i in range(far)])
    packed = call(
        lambda *refs: spread_kernel(blocks, *refs),
        shape((count * ROLES, LANES), BF16),
        [VMEM] * 4,
        [rows],
    )(gate, d_in, filt, beside)
    packed = lax.all_to_all(packed, ("near", "seq"), 0, 0, tiled=True)
    d_input, d_gate, d_filter = call(
        unpack_kernel,
        (shape((chans, LANES), BF16), shape((chans, LANES), BF16), shape((chans, LANES), F32)),
        [VMEM],
        [pltpu.VMEM((chans * ROLES, LANES), F32)],
    )(packed)
    return d_input[None], d_gate[None], d_filter


def solution(mesh):
    sizes = mesh.devices.shape
    mesh = Mesh(mesh.devices.reshape(sizes[0] // GROUP, GROUP, sizes[1]), ("far", "near", "seq"))
    signal = P(("far", "near"), None, "seq")
    return jax.shard_map(
        body,
        mesh=mesh,
        in_specs=(signal, signal, signal, P(None, "seq"), P()),
        out_specs=(signal, signal, P(None, "seq")),
        check_vma=False,
    )
```

```python
import jax
import jax.numpy as jnp
from jax import lax
from jax.experimental import pallas as pl
from jax.experimental.pallas import tpu as pltpu
from jax.sharding import Mesh, PartitionSpec as P

LANES = 128
GROUP = 4
ROLES = 4

F32 = jnp.float32
BF16 = jnp.bfloat16


def iota(shape, dim):
    return lax.broadcasted_iota(jnp.int32, shape, dim)


def pack_kernel(u_ref, g_ref, y_ref, k_ref, out_ref, landed, rows, sems):
    chans = out_ref.shape[0] // ROLES
    copies = [
        pltpu.make_async_copy(ref, landed.at[role], sems.at[role])
        for role, ref in enumerate((u_ref, g_ref, y_ref, k_ref))
    ]
    for copy in copies:
        copy.start()
    for role, copy in enumerate(copies):
        copy.wait()
        rows[pl.ds(role, chans, stride=ROLES), :] = landed[role].astype(F32)
    out_ref[...] = rows[...].astype(BF16)


def flip_rows(count, span):
    row, col = iota((count, count), 0), iota((count, count), 1)
    same = row // span == col // span
    return jnp.where(same & (row % span + col % span == span - 1), 1.0, 0.0).astype(BF16)


def take(rows, role, count):
    return rows[pl.ds(role, count, stride=ROLES), :]


def flipped_pair(gc, flip, lane_flip):
    high = gc.astype(BF16)
    low = (gc - high.astype(F32)).astype(BF16)
    both = jnp.concatenate([high, low], axis=0)
    both = jnp.dot(both, lane_flip, preferred_element_type=F32).astype(BF16)
    return jnp.dot(flip, both, preferred_element_type=F32)


def pad(padded, value, blocks):
    for part in range(padded.shape[0]):
        padded[part, :blocks, :] = jnp.zeros((blocks, LANES), F32)
        padded[part, blocks:, :] = value[part * blocks : (part + 1) * blocks]


def shifted(padded, d, blocks):
    parts = [padded[part, blocks - d : 2 * blocks - d, :] for part in range(padded.shape[0])]
    return jnp.concatenate(parts, axis=0).astype(BF16)


def skew(value):
    return pltpu.roll(value, 0, 1, stride=1, stride_axis=0)


def filt_kernel(blocks, in_ref, filt_ref, rows, padded, filt_rows):
    count = GROUP * blocks
    rows[...] = in_ref[...].astype(F32)
    u = take(rows, 0, count)
    gc = take(rows, 1, count) * take(rows, 2, count)
    lane_flip = flip_rows(LANES, LANES)
    flip = flip_rows(2 * count, blocks)
    pad(padded, flipped_pair(gc, flip, lane_flip), blocks)
    turned_u = jnp.dot(flip[:count, :count], u.astype(BF16), preferred_element_type=F32)
    left = jnp.transpose(turned_u).astype(BF16)
    left = jnp.concatenate([left, left], axis=1)
    inside = iota((LANES, LANES), 1) >= iota((LANES, LANES), 0)
    held = None
    for pair in range(blocks // 2):
        wide = jnp.concatenate([shifted(padded, 2 * pair, blocks), shifted(padded, 2 * pair + 1, blocks)], axis=1)
        products = jnp.dot(left, wide, preferred_element_type=F32)
        for half in range(2):
            d = 2 * pair + half
            turned = skew(products[:, half * LANES : (half + 1) * LANES])
            if held is not None:
                filt_rows[d - 1 : d, :] = jnp.sum(jnp.where(inside, held, turned), axis=0, keepdims=True)
            held = turned
    filt_rows[blocks - 1 : blocks, :] = jnp.sum(jnp.where(inside, held, 0.0), axis=0, keepdims=True)
    filt_ref[...] = jnp.dot(
        filt_rows[...], lane_flip.astype(F32), precision=lax.Precision.HIGHEST, preferred_element_type=F32
    )


def conv_kernel(blocks, chan_ref, gain_ref, in_ref, gate_ref, input_ref, rows, padded, gains, sem):
    count = GROUP * blocks
    fetch = pltpu.make_async_copy(gain_ref, gains, sem)
    fetch.start()
    rows[...] = in_ref[...].astype(F32)
    u = take(rows, 0, count)
    y = take(rows, 2, count)
    gc = take(rows, 1, count) * y
    k = take(rows, 3, blocks)
    lane_flip = flip_rows(LANES, LANES)
    flip = flip_rows(2 * count, blocks)
    both = flipped_pair(gc, flip, lane_flip)
    pad(padded, jnp.concatenate([u, both], axis=0), blocks)
    inside = iota((LANES, LANES), 1) >= iota((LANES, LANES), 0)
    before = jnp.zeros((LANES, LANES), F32)
    total = jnp.zeros((3 * count, LANES), F32)
    for pair in range(blocks // 2):
        signal, toeplitz = [], []
        for d in (2 * pair, 2 * pair + 1):
            signal.append(shifted(padded, d, blocks))
            rolled = skew(jnp.broadcast_to(k[d : d + 1, :], (LANES, LANES)))
            toeplitz.append(jnp.where(inside, rolled, before).astype(BF16))
            before = rolled
        total = total + jnp.dot(
            jnp.concatenate(signal, axis=1), jnp.concatenate(toeplitz, axis=0), preferred_element_type=F32
        )
    scale = 1.0 / 64.0
    fetch.wait()
    gain = gains[chan_ref[0]]
    gate_ref[...] = (y * (total[:count] * scale + gain * u)).astype(BF16)
    corr = total[count : 2 * count] + total[2 * count :]
    d_input = (corr * scale + gain * (both[:count] + both[count:])).astype(BF16)
    d_input = jnp.dot(d_input, lane_flip, preferred_element_type=F32).astype(BF16)
    input_ref[...] = jnp.dot(flip[:count, :count], d_input, preferred_element_type=F32).astype(BF16)


def spread_kernel(blocks, gate_ref, input_ref, near_ref, far_ref, out_ref, rows):
    count = GROUP * blocks
    filt = near_ref[...] + far_ref[...]
    high = filt.astype(BF16).astype(F32)
    low = filt - high
    rows[pl.ds(0, count, stride=ROLES), :] = gate_ref[...].astype(F32)
    rows[pl.ds(1, count, stride=ROLES), :] = input_ref[...].astype(F32)
    for part in range(GROUP):
        at = part * blocks * ROLES
        rows[pl.ds(at + 2, blocks, stride=ROLES), :] = high
        rows[pl.ds(at + 3, blocks, stride=ROLES), :] = low
    out_ref[...] = rows[...].astype(BF16)


def unpack_kernel(in_ref, input_ref, gate_ref, filt_ref, rows):
    chans = input_ref.shape[0]
    rows[...] = in_ref[...].astype(F32)
    gate_ref[...] = take(rows, 0, chans).astype(BF16)
    input_ref[...] = take(rows, 1, chans).astype(BF16)
    filt_ref[...] = (take(rows, 2, chans) + take(rows, 3, chans)) * (1.0 / 64.0)


VMEM = pl.BlockSpec(memory_space=pltpu.VMEM)
SMEM = pl.BlockSpec(memory_space=pltpu.SMEM)


def shape(dims, dtype):
    return jax.ShapeDtypeStruct(dims, dtype)


HBM = pl.BlockSpec(memory_space=pltpu.HBM)


def call(kernel, outs, ins, scratch, limit=48):
    return pl.pallas_call(
        kernel,
        out_shape=outs,
        in_specs=ins,
        out_specs=jax.tree.map(lambda _: VMEM, outs),
        scratch_shapes=scratch,
        compiler_params=pltpu.CompilerParams(vmem_limit_bytes=limit * 1024 * 1024),
    )


def body(inputs, gate_values, grad_out, filter_raw, skip_gain):
    blocks = lax.axis_size("seq")
    far = lax.axis_size("far")
    chans = inputs.shape[1]
    count = GROUP * blocks
    rows = pltpu.VMEM((count * ROLES, LANES), F32)
    packed = call(
        pack_kernel,
        shape((chans * ROLES, LANES), BF16),
        [HBM] * 4,
        [
            pltpu.VMEM((ROLES, chans, LANES), BF16),
            pltpu.VMEM((chans * ROLES, LANES), F32),
            pltpu.SemaphoreType.DMA((ROLES,)),
        ],
        60,
    )(inputs[0], gate_values[0], grad_out[0], filter_raw)
    packed = lax.all_to_all(packed, ("near", "seq"), 0, 0, tiled=True)
    filt = call(
        lambda *refs: filt_kernel(blocks, *refs),
        shape((blocks, LANES), F32),
        [VMEM],
        [rows, pltpu.VMEM((2 * GROUP, 2 * blocks, LANES), F32), pltpu.VMEM((blocks, LANES), F32)],
    )(packed)
    around = lax.ppermute(filt, "far", [(i, i ^ 3) for i in range(far)])
    chan = (lax.axis_index("near") * blocks + lax.axis_index("seq")).reshape(1)
    gate, d_in = call(
        lambda *refs: conv_kernel(blocks, *refs),
        (shape((count, LANES), BF16), shape((count, LANES), BF16)),
        [SMEM, HBM, VMEM],
        [
            rows,
            pltpu.VMEM((3 * GROUP, 2 * blocks, LANES), F32),
            pltpu.SMEM(skip_gain.shape, F32),
            pltpu.SemaphoreType.DMA(()),
        ],
    )(chan, skip_gain, packed)
    filt = filt + around
    beside = lax.ppermute(filt, "far", [(i, i ^ 1) for i in range(far)])
    packed = call(
        lambda *refs: spread_kernel(blocks, *refs),
        shape((count * ROLES, LANES), BF16),
        [VMEM] * 4,
        [rows],
    )(gate, d_in, filt, beside)
    packed = lax.all_to_all(packed, ("near", "seq"), 0, 0, tiled=True)
    d_input, d_gate, d_filter = call(
        unpack_kernel,
        (shape((chans, LANES), BF16), shape((chans, LANES), BF16), shape((chans, LANES), F32)),
        [VMEM],
        [pltpu.VMEM((chans * ROLES, LANES), F32)],
    )(packed)
    return d_input[None], d_gate[None], d_filter


def solution(mesh):
    sizes = mesh.devices.shape
    mesh = Mesh(mesh.devices.reshape(sizes[0] // GROUP, GROUP, sizes[1]), ("far", "near", "seq"))
    signal = P(("far", "near"), None, "seq")
    return jax.shard_map(
        body,
        mesh=mesh,
        in_specs=(signal, signal, signal, P(None, "seq"), P()),
        out_specs=(signal, signal, P(None, "seq")),
        check_vma=False,
    )
```

```python
import jax
import jax.numpy as jnp
from jax import lax
from jax.experimental import pallas as pl
from jax.experimental.pallas import tpu as pltpu
from jax.sharding import Mesh, PartitionSpec as P

LANES = 128
GROUP = 4
ROLES = 4

F32 = jnp.float32
BF16 = jnp.bfloat16


def iota(shape, dim):
    return lax.broadcasted_iota(jnp.int32, shape, dim)


def pack_kernel(u_ref, g_ref, y_ref, k_ref, out_ref, landed, rows, sems):
    chans = out_ref.shape[0] // ROLES
    copies = [
        pltpu.make_async_copy(ref, landed.at[role], sems.at[role])
        for role, ref in enumerate((u_ref, g_ref, y_ref, k_ref))
    ]
    for copy in copies:
        copy.start()
    for role, copy in enumerate(copies):
        copy.wait()
        rows[pl.ds(role, chans, stride=ROLES), :] = landed[role].astype(F32)
    out_ref[...] = rows[...].astype(BF16)


def flip_rows(count, span):
    row, col = iota((count, count), 0), iota((count, count), 1)
    same = row // span == col // span
    return jnp.where(same & (row % span + col % span == span - 1), 1.0, 0.0).astype(BF16)


def take(rows, role, count):
    return rows[pl.ds(role, count, stride=ROLES), :]


def flipped_pair(gc, flip, lane_flip):
    high = gc.astype(BF16)
    low = (gc - high.astype(F32)).astype(BF16)
    both = jnp.concatenate([high, low], axis=0)
    both = jnp.dot(both, lane_flip, preferred_element_type=F32).astype(BF16)
    return jnp.dot(flip, both, preferred_element_type=F32)


def pad(padded, value, blocks):
    for part in range(padded.shape[0]):
        padded[part, :blocks, :] = jnp.zeros((blocks, LANES), F32)
        padded[part, blocks:, :] = value[part * blocks : (part + 1) * blocks]


def shifted(padded, d, blocks):
    parts = [padded[part, blocks - d : 2 * blocks - d, :] for part in range(padded.shape[0])]
    return jnp.concatenate(parts, axis=0).astype(BF16)


def skew(value):
    return pltpu.roll(value, 0, 1, stride=1, stride_axis=0)


def filt_kernel(blocks, in_ref, filt_ref, rows, padded):
    count = GROUP * blocks
    rows[...] = in_ref[...].astype(F32)
    u = take(rows, 0, count)
    gc = take(rows, 1, count) * take(rows, 2, count)
    high = gc.astype(BF16).astype(F32)
    low = gc - high
    for part in range(2 * GROUP):
        value = high if part < GROUP else low
        at = part % GROUP * blocks
        padded[part, :blocks, :] = value[at : at + blocks]
        padded[part, blocks:, :] = jnp.zeros((blocks, LANES), F32)
    left = lax.dot_general(
        flip_rows(LANES, LANES), u.astype(BF16), (((1,), (1,)), ((), ())), preferred_element_type=F32
    ).astype(BF16)
    left = jnp.concatenate([left, left], axis=1)
    wrapped = iota((LANES, LANES), 1) <= iota((LANES, LANES), 0)
    held = None
    for pair in range(blocks // 2):
        wide = []
        for d in (2 * pair, 2 * pair + 1):
            parts = [padded[part, d : d + blocks, :] for part in range(2 * GROUP)]
            wide.append(jnp.concatenate(parts, axis=0).astype(BF16))
        products = jnp.dot(left, jnp.concatenate(wide, axis=1), preferred_element_type=F32)
        for half in range(2):
            d = 2 * pair + half
            turned = pltpu.roll(products[:, half * LANES : (half + 1) * LANES], 1, 1, stride=1, stride_axis=0)
            if held is not None:
                filt_ref[d - 1 : d, :] = jnp.sum(jnp.where(wrapped, held, turned), axis=0, keepdims=True)
            held = turned
    filt_ref[blocks - 1 : blocks, :] = jnp.sum(jnp.where(wrapped, held, 0.0), axis=0, keepdims=True)


def conv_kernel(blocks, chan_ref, gain_ref, in_ref, gate_ref, input_ref, rows, padded, gains, sem):
    count = GROUP * blocks
    fetch = pltpu.make_async_copy(gain_ref, gains, sem)
    fetch.start()
    rows[...] = in_ref[...].astype(F32)
    u = take(rows, 0, count)
    y = take(rows, 2, count)
    gc = take(rows, 1, count) * y
    k = take(rows, 3, blocks)
    lane_flip = flip_rows(LANES, LANES)
    flip = flip_rows(2 * count, blocks)
    both = flipped_pair(gc, flip, lane_flip)
    pad(padded, jnp.concatenate([u, both], axis=0), blocks)
    inside = iota((LANES, LANES), 1) >= iota((LANES, LANES), 0)
    before = jnp.zeros((LANES, LANES), F32)
    total = jnp.zeros((3 * count, LANES), F32)
    for pair in range(blocks // 2):
        signal, toeplitz = [], []
        for d in (2 * pair, 2 * pair + 1):
            signal.append(shifted(padded, d, blocks))
            rolled = skew(jnp.broadcast_to(k[d : d + 1, :], (LANES, LANES)))
            toeplitz.append(jnp.where(inside, rolled, before).astype(BF16))
            before = rolled
        total = total + jnp.dot(
            jnp.concatenate(signal, axis=1), jnp.concatenate(toeplitz, axis=0), preferred_element_type=F32
        )
    scale = 1.0 / 64.0
    fetch.wait()
    gain = gains[chan_ref[0]]
    gate_ref[...] = (y * (total[:count] * scale + gain * u)).astype(BF16)
    corr = total[count : 2 * count] + total[2 * count :]
    d_input = (corr * scale + gain * (both[:count] + both[count:])).astype(BF16)
    d_input = jnp.dot(d_input, lane_flip, preferred_element_type=F32).astype(BF16)
    input_ref[...] = jnp.dot(flip[:count, :count], d_input, preferred_element_type=F32).astype(BF16)


def spread_kernel(blocks, gate_ref, input_ref, near_ref, far_ref, out_ref, rows):
    count = GROUP * blocks
    filt = near_ref[...] + far_ref[...]
    high = filt.astype(BF16).astype(F32)
    low = filt - high
    rows[pl.ds(0, count, stride=ROLES), :] = gate_ref[...].astype(F32)
    rows[pl.ds(1, count, stride=ROLES), :] = input_ref[...].astype(F32)
    for part in range(GROUP):
        at = part * blocks * ROLES
        rows[pl.ds(at + 2, blocks, stride=ROLES), :] = high
        rows[pl.ds(at + 3, blocks, stride=ROLES), :] = low
    out_ref[...] = rows[...].astype(BF16)


def unpack_kernel(in_ref, input_ref, gate_ref, filt_ref, rows):
    chans = input_ref.shape[0]
    rows[...] = in_ref[...].astype(F32)
    gate_ref[...] = take(rows, 0, chans).astype(BF16)
    input_ref[...] = take(rows, 1, chans).astype(BF16)
    filt_ref[...] = (take(rows, 2, chans) + take(rows, 3, chans)) * (1.0 / 64.0)


VMEM = pl.BlockSpec(memory_space=pltpu.VMEM)
SMEM = pl.BlockSpec(memory_space=pltpu.SMEM)


def shape(dims, dtype):
    return jax.ShapeDtypeStruct(dims, dtype)


HBM = pl.BlockSpec(memory_space=pltpu.HBM)


def in_hbm(array):
    return pltpu.with_memory_space_constraint(array, pltpu.HBM)


def call(kernel, outs, ins, scratch):
    return pl.pallas_call(
        kernel,
        out_shape=outs,
        in_specs=ins,
        out_specs=jax.tree.map(lambda _: VMEM, outs),
        scratch_shapes=scratch,
        compiler_params=pltpu.CompilerParams(vmem_limit_bytes=48 * 1024 * 1024),
    )


def body(inputs, gate_values, grad_out, filter_raw, skip_gain):
    blocks = lax.axis_size("seq")
    far = lax.axis_size("far")
    chans = inputs.shape[1]
    count = GROUP * blocks
    rows = pltpu.VMEM((count * ROLES, LANES), F32)
    packed = call(
        pack_kernel,
        shape((chans * ROLES, LANES), BF16),
        [HBM] * 4,
        [
            pltpu.VMEM((ROLES, chans, LANES), BF16),
            pltpu.VMEM((chans * ROLES, LANES), F32),
            pltpu.SemaphoreType.DMA((ROLES,)),
        ],
    )(*map(in_hbm, (inputs[0], gate_values[0], grad_out[0], filter_raw)))
    packed = lax.all_to_all(packed, ("near", "seq"), 0, 0, tiled=True)
    filt = call(
        lambda *refs: filt_kernel(blocks, *refs),
        shape((blocks, LANES), F32),
        [VMEM],
        [rows, pltpu.VMEM((2 * GROUP, 2 * blocks, LANES), F32)],
    )(packed)
    around = lax.ppermute(filt, "far", [(i, i ^ 3) for i in range(far)])
    chan = (lax.axis_index("near") * blocks + lax.axis_index("seq")).reshape(1)
    gate, d_in = call(
        lambda *refs: conv_kernel(blocks, *refs),
        (shape((count, LANES), BF16), shape((count, LANES), BF16)),
        [SMEM, HBM, VMEM],
        [
            rows,
            pltpu.VMEM((3 * GROUP, 2 * blocks, LANES), F32),
            pltpu.SMEM(skip_gain.shape, F32),
            pltpu.SemaphoreType.DMA(()),
        ],
    )(chan, in_hbm(skip_gain), packed)
    filt = filt + around
    beside = lax.ppermute(filt, "far", [(i, i ^ 1) for i in range(far)])
    packed = call(
        lambda *refs: spread_kernel(blocks, *refs),
        shape((count * ROLES, LANES), BF16),
        [VMEM] * 4,
        [rows],
    )(gate, d_in, filt, beside)
    packed = lax.all_to_all(packed, ("near", "seq"), 0, 0, tiled=True)
    d_input, d_gate, d_filter = call(
        unpack_kernel,
        (shape((chans, LANES), BF16), shape((chans, LANES), BF16), shape((chans, LANES), F32)),
        [VMEM],
        [pltpu.VMEM((chans * ROLES, LANES), F32)],
    )(packed)
    return d_input[None], d_gate[None], d_filter


def solution(mesh):
    sizes = mesh.devices.shape
    mesh = Mesh(mesh.devices.reshape(sizes[0] // GROUP, GROUP, sizes[1]), ("far", "near", "seq"))
    signal = P(("far", "near"), None, "seq")
    return jax.shard_map(
        body,
        mesh=mesh,
        in_specs=(signal, signal, signal, P(None, "seq"), P()),
        out_specs=(signal, signal, P(None, "seq")),
        check_vma=False,
    )
```

```python
import jax
import jax.numpy as jnp
from jax import lax
from jax.experimental import pallas as pl
from jax.experimental.pallas import tpu as pltpu
from jax.sharding import Mesh, PartitionSpec as P

LANES = 128
GROUP = 4
ROLES = 4

F32 = jnp.float32
BF16 = jnp.bfloat16


def iota(shape, dim):
    return lax.broadcasted_iota(jnp.int32, shape, dim)


def swapped(value, odd):
    up, down = jnp.roll(value, -1, axis=0), jnp.roll(value, 1, axis=0)
    other = jnp.where(iota(value.shape, 0) % 2 == 0, up, down)
    return jnp.where(odd, other, value)


def pack_kernel(far_ref, u_ref, g_ref, y_ref, k_ref, out_ref, landed, rows, sems):
    chans = out_ref.shape[0] // ROLES
    copies = [
        pltpu.make_async_copy(ref, landed.at[role], sems.at[role])
        for role, ref in enumerate((u_ref, g_ref, y_ref, k_ref))
    ]
    for copy in copies:
        copy.start()
    odd = far_ref[0] % 2 == 1
    for role, copy in enumerate(copies):
        copy.wait()
        rows[pl.ds(role, chans, stride=ROLES), :] = swapped(landed[role].astype(F32), odd)
    out_ref[...] = rows[...].astype(BF16)


def flip_rows(count, span):
    row, col = iota((count, count), 0), iota((count, count), 1)
    same = row // span == col // span
    return jnp.where(same & (row % span + col % span == span - 1), 1.0, 0.0).astype(BF16)


def take(rows, role, count):
    return rows[pl.ds(role, count, stride=ROLES), :]


def flipped_pair(gc, flip, lane_flip):
    high = gc.astype(BF16)
    low = (gc - high.astype(F32)).astype(BF16)
    both = jnp.concatenate([high, low], axis=0)
    both = jnp.dot(both, lane_flip, preferred_element_type=F32).astype(BF16)
    return jnp.dot(flip, both, preferred_element_type=F32)


def pad(padded, value, blocks):
    for part in range(padded.shape[0]):
        padded[part, :blocks, :] = jnp.zeros((blocks, LANES), F32)
        padded[part, blocks:, :] = value[part * blocks : (part + 1) * blocks]


def shifted(padded, d, blocks):
    parts = [padded[part, blocks - d : 2 * blocks - d, :] for part in range(padded.shape[0])]
    return jnp.concatenate(parts, axis=0).astype(BF16)


def skew(value):
    return pltpu.roll(value, 0, 1, stride=1, stride_axis=0)


def filt_kernel(blocks, in_ref, filt_ref, rows, padded):
    count = GROUP * blocks
    rows[...] = in_ref[...].astype(F32)
    u = take(rows, 0, count)
    gc = take(rows, 1, count) * take(rows, 2, count)
    high = gc.astype(BF16).astype(F32)
    low = gc - high
    for part in range(2 * GROUP):
        value = high if part < GROUP else low
        at = part % GROUP * blocks
        padded[part, :blocks, :] = value[at : at + blocks]
        padded[part, blocks:, :] = jnp.zeros((blocks, LANES), F32)
    left = lax.dot_general(
        flip_rows(LANES, LANES), u.astype(BF16), (((1,), (1,)), ((), ())), preferred_element_type=F32
    ).astype(BF16)
    left = jnp.concatenate([left, left], axis=1)
    wrapped = iota((LANES, LANES), 1) <= iota((LANES, LANES), 0)
    held = None
    for pair in range(blocks // 2):
        wide = []
        for d in (2 * pair, 2 * pair + 1):
            parts = [padded[part, d : d + blocks, :] for part in range(2 * GROUP)]
            wide.append(jnp.concatenate(parts, axis=0).astype(BF16))
        products = jnp.dot(left, jnp.concatenate(wide, axis=1), preferred_element_type=F32)
        for half in range(2):
            d = 2 * pair + half
            turned = pltpu.roll(products[:, half * LANES : (half + 1) * LANES], 1, 1, stride=1, stride_axis=0)
            if held is not None:
                filt_ref[d - 1 : d, :] = jnp.sum(jnp.where(wrapped, held, turned), axis=0, keepdims=True)
            held = turned
    filt_ref[blocks - 1 : blocks, :] = jnp.sum(jnp.where(wrapped, held, 0.0), axis=0, keepdims=True)


def conv_kernel(blocks, chan_ref, gain_ref, in_ref, gate_ref, input_ref, rows, padded, gains, sem):
    count = GROUP * blocks
    fetch = pltpu.make_async_copy(gain_ref, gains, sem)
    fetch.start()
    rows[...] = in_ref[...].astype(F32)
    u = take(rows, 0, count)
    y = take(rows, 2, count)
    gc = take(rows, 1, count) * y
    k = take(rows, 3, blocks)
    lane_flip = flip_rows(LANES, LANES)
    flip = flip_rows(2 * count, blocks)
    both = flipped_pair(gc, flip, lane_flip)
    pad(padded, jnp.concatenate([u, both], axis=0), blocks)
    inside = iota((LANES, LANES), 1) >= iota((LANES, LANES), 0)
    before = jnp.zeros((LANES, LANES), F32)
    total = jnp.zeros((3 * count, LANES), F32)
    for pair in range(blocks // 2):
        signal, toeplitz = [], []
        for d in (2 * pair, 2 * pair + 1):
            signal.append(shifted(padded, d, blocks))
            rolled = skew(jnp.broadcast_to(k[d : d + 1, :], (LANES, LANES)))
            toeplitz.append(jnp.where(inside, rolled, before).astype(BF16))
            before = rolled
        total = total + jnp.dot(
            jnp.concatenate(signal, axis=1), jnp.concatenate(toeplitz, axis=0), preferred_element_type=F32
        )
    scale = 1.0 / 64.0
    fetch.wait()
    gain = gains[chan_ref[0]]
    gate_ref[...] = (y * (total[:count] * scale + gain * u)).astype(BF16)
    corr = total[count : 2 * count] + total[2 * count :]
    d_input = (corr * scale + gain * (both[:count] + both[count:])).astype(BF16)
    d_input = jnp.dot(d_input, lane_flip, preferred_element_type=F32).astype(BF16)
    input_ref[...] = jnp.dot(flip[:count, :count], d_input, preferred_element_type=F32).astype(BF16)


def spread_kernel(blocks, gate_ref, input_ref, near_ref, far_ref, out_ref, rows):
    count = GROUP * blocks
    filt = near_ref[...] + far_ref[...]
    high = filt.astype(BF16).astype(F32)
    low = filt - high
    rows[pl.ds(0, count, stride=ROLES), :] = gate_ref[...].astype(F32)
    rows[pl.ds(1, count, stride=ROLES), :] = input_ref[...].astype(F32)
    for part in range(GROUP):
        at = part * blocks * ROLES
        rows[pl.ds(at + 2, blocks, stride=ROLES), :] = high
        rows[pl.ds(at + 3, blocks, stride=ROLES), :] = low
    out_ref[...] = rows[...].astype(BF16)


def unpack_kernel(far_ref, in_ref, input_ref, gate_ref, filt_ref, rows):
    chans = input_ref.shape[0]
    odd = far_ref[0] % 2 == 1
    rows[...] = in_ref[...].astype(F32)
    gate_ref[...] = swapped(take(rows, 0, chans), odd).astype(BF16)
    input_ref[...] = swapped(take(rows, 1, chans), odd).astype(BF16)
    filt_ref[...] = swapped(take(rows, 2, chans) + take(rows, 3, chans), odd) * (1.0 / 64.0)


VMEM = pl.BlockSpec(memory_space=pltpu.VMEM)
SMEM = pl.BlockSpec(memory_space=pltpu.SMEM)


def shape(dims, dtype):
    return jax.ShapeDtypeStruct(dims, dtype)


HBM = pl.BlockSpec(memory_space=pltpu.HBM)


def in_hbm(array):
    return pltpu.with_memory_space_constraint(array, pltpu.HBM)


def call(kernel, outs, ins, scratch):
    return pl.pallas_call(
        kernel,
        out_shape=outs,
        in_specs=ins,
        out_specs=jax.tree.map(lambda _: VMEM, outs),
        scratch_shapes=scratch,
        compiler_params=pltpu.CompilerParams(vmem_limit_bytes=48 * 1024 * 1024),
    )


def exchange(array, step):
    far, seq = lax.axis_size("far"), lax.axis_size("seq")
    pairs = [(i * seq + j, (i ^ step) * seq + (j ^ 1)) for i in range(far) for j in range(seq)]
    return lax.ppermute(array, ("far", "seq"), pairs)


def body(inputs, gate_values, grad_out, filter_raw, skip_gain):
    blocks = lax.axis_size("seq")
    far = lax.axis_index("far").reshape(1)
    chans = inputs.shape[1]
    count = GROUP * blocks
    rows = pltpu.VMEM((count * ROLES, LANES), F32)
    packed = call(
        pack_kernel,
        shape((chans * ROLES, LANES), BF16),
        [SMEM] + [HBM] * 4,
        [
            pltpu.VMEM((ROLES, chans, LANES), BF16),
            pltpu.VMEM((chans * ROLES, LANES), F32),
            pltpu.SemaphoreType.DMA((ROLES,)),
        ],
    )(far, *map(in_hbm, (inputs[0], gate_values[0], grad_out[0], filter_raw)))
    packed = lax.all_to_all(packed, ("near", "seq"), 0, 0, tiled=True)
    filt = call(
        lambda *refs: filt_kernel(blocks, *refs),
        shape((blocks, LANES), F32),
        [VMEM],
        [rows, pltpu.VMEM((2 * GROUP, 2 * blocks, LANES), F32)],
    )(packed)
    around = exchange(filt, 3)
    chan = lax.axis_index("near") * blocks + (lax.axis_index("seq") ^ (far & 1))
    gate, d_in = call(
        lambda *refs: conv_kernel(blocks, *refs),
        (shape((count, LANES), BF16), shape((count, LANES), BF16)),
        [SMEM, HBM, VMEM],
        [
            rows,
            pltpu.VMEM((3 * GROUP, 2 * blocks, LANES), F32),
            pltpu.SMEM(skip_gain.shape, F32),
            pltpu.SemaphoreType.DMA(()),
        ],
    )(chan, in_hbm(skip_gain), packed)
    filt = filt + around
    beside = exchange(filt, 1)
    packed = call(
        lambda *refs: spread_kernel(blocks, *refs),
        shape((count * ROLES, LANES), BF16),
        [VMEM] * 4,
        [rows],
    )(gate, d_in, filt, beside)
    packed = lax.all_to_all(packed, ("near", "seq"), 0, 0, tiled=True)
    d_input, d_gate, d_filter = call(
        unpack_kernel,
        (shape((chans, LANES), BF16), shape((chans, LANES), BF16), shape((chans, LANES), F32)),
        [SMEM, VMEM],
        [pltpu.VMEM((chans * ROLES, LANES), F32)],
    )(far, packed)
    return d_input[None], d_gate[None], d_filter


def solution(mesh):
    sizes = mesh.devices.shape
    mesh = Mesh(mesh.devices.reshape(sizes[0] // GROUP, GROUP, sizes[1]), ("far", "near", "seq"))
    signal = P(("far", "near"), None, "seq")
    return jax.shard_map(
        body,
        mesh=mesh,
        in_specs=(signal, signal, signal, P(None, "seq"), P()),
        out_specs=(signal, signal, P(None, "seq")),
        check_vma=False,
    )
```

```python
import jax
import jax.numpy as jnp
from jax import lax
from jax.experimental import pallas as pl
from jax.experimental.pallas import tpu as pltpu
from jax.sharding import Mesh, PartitionSpec as P

LANES = 128
GROUP = 4
ROLES = 4

F32 = jnp.float32
BF16 = jnp.bfloat16


def iota(shape, dim):
    return lax.broadcasted_iota(jnp.int32, shape, dim)


def swapped(value, odd):
    up, down = jnp.roll(value, -1, axis=0), jnp.roll(value, 1, axis=0)
    other = jnp.where(iota(value.shape, 0) % 2 == 0, up, down)
    return jnp.where(odd, other, value)


def pack_kernel(far_ref, u_ref, g_ref, y_ref, k_ref, out_ref, landed, rows, sems):
    chans = out_ref.shape[0] // ROLES
    copies = [
        pltpu.make_async_copy(ref, landed.at[role], sems.at[role])
        for role, ref in enumerate((u_ref, g_ref, y_ref, k_ref))
    ]
    for copy in copies:
        copy.start()
    odd = swaps(far_ref[0]) == 1
    for role, copy in enumerate(copies):
        copy.wait()
        rows[pl.ds(role, chans, stride=ROLES), :] = swapped(landed[role].astype(F32), odd)
    out_ref[...] = rows[...].astype(BF16)


def flip_rows(count, span):
    row, col = iota((count, count), 0), iota((count, count), 1)
    same = row // span == col // span
    return jnp.where(same & (row % span + col % span == span - 1), 1.0, 0.0).astype(BF16)


def take(rows, role, count):
    return rows[pl.ds(role, count, stride=ROLES), :]


def flipped_pair(gc, flip, lane_flip):
    high = gc.astype(BF16)
    low = (gc - high.astype(F32)).astype(BF16)
    both = jnp.concatenate([high, low], axis=0)
    both = jnp.dot(both, lane_flip, preferred_element_type=F32).astype(BF16)
    return jnp.dot(flip, both, preferred_element_type=F32)


def pad(padded, value, blocks):
    for part in range(padded.shape[0]):
        padded[part, :blocks, :] = jnp.zeros((blocks, LANES), F32)
        padded[part, blocks:, :] = value[part * blocks : (part + 1) * blocks]


def shifted(padded, d, blocks):
    parts = [padded[part, blocks - d : 2 * blocks - d, :] for part in range(padded.shape[0])]
    return jnp.concatenate(parts, axis=0).astype(BF16)


def skew(value):
    return pltpu.roll(value, 0, 1, stride=1, stride_axis=0)


def filt_kernel(blocks, in_ref, filt_ref, rows, padded):
    count = GROUP * blocks
    rows[...] = in_ref[...].astype(F32)
    u = take(rows, 0, count)
    gc = take(rows, 1, count) * take(rows, 2, count)
    high = gc.astype(BF16).astype(F32)
    low = gc - high
    for part in range(2 * GROUP):
        value = high if part < GROUP else low
        at = part % GROUP * blocks
        padded[part, :blocks, :] = value[at : at + blocks]
        padded[part, blocks:, :] = jnp.zeros((blocks, LANES), F32)
    left = lax.dot_general(
        flip_rows(LANES, LANES), u.astype(BF16), (((1,), (1,)), ((), ())), preferred_element_type=F32
    ).astype(BF16)
    left = jnp.concatenate([left, left], axis=1)
    wrapped = iota((LANES, LANES), 1) <= iota((LANES, LANES), 0)
    held = None
    for pair in range(blocks // 2):
        wide = []
        for d in (2 * pair, 2 * pair + 1):
            parts = [padded[part, d : d + blocks, :] for part in range(2 * GROUP)]
            wide.append(jnp.concatenate(parts, axis=0).astype(BF16))
        products = jnp.dot(left, jnp.concatenate(wide, axis=1), preferred_element_type=F32)
        for half in range(2):
            d = 2 * pair + half
            turned = pltpu.roll(products[:, half * LANES : (half + 1) * LANES], 1, 1, stride=1, stride_axis=0)
            if held is not None:
                filt_ref[d - 1 : d, :] = jnp.sum(jnp.where(wrapped, held, turned), axis=0, keepdims=True)
            held = turned
    filt_ref[blocks - 1 : blocks, :] = jnp.sum(jnp.where(wrapped, held, 0.0), axis=0, keepdims=True)


def conv_kernel(blocks, chan_ref, gain_ref, in_ref, filt_ref, gate_ref, input_ref, same_ref, rows, padded, gains, sem):
    count = GROUP * blocks
    fetch = pltpu.make_async_copy(gain_ref, gains, sem)
    fetch.start()
    same_ref[...] = filt_ref[...]
    rows[...] = in_ref[...].astype(F32)
    u = take(rows, 0, count)
    y = take(rows, 2, count)
    gc = take(rows, 1, count) * y
    k = take(rows, 3, blocks)
    lane_flip = flip_rows(LANES, LANES)
    flip = flip_rows(2 * count, blocks)
    both = flipped_pair(gc, flip, lane_flip)
    pad(padded, jnp.concatenate([u, both], axis=0), blocks)
    inside = iota((LANES, LANES), 1) >= iota((LANES, LANES), 0)
    before = jnp.zeros((LANES, LANES), F32)
    total = jnp.zeros((3 * count, LANES), F32)
    for pair in range(blocks // 2):
        signal, toeplitz = [], []
        for d in (2 * pair, 2 * pair + 1):
            signal.append(shifted(padded, d, blocks))
            rolled = skew(jnp.broadcast_to(k[d : d + 1, :], (LANES, LANES)))
            toeplitz.append(jnp.where(inside, rolled, before).astype(BF16))
            before = rolled
        total = total + jnp.dot(
            jnp.concatenate(signal, axis=1), jnp.concatenate(toeplitz, axis=0), preferred_element_type=F32
        )
    scale = 1.0 / 64.0
    fetch.wait()
    gain = gains[chan_ref[0]]
    gate_ref[...] = (y * (total[:count] * scale + gain * u)).astype(BF16)
    corr = total[count : 2 * count] + total[2 * count :]
    d_input = (corr * scale + gain * (both[:count] + both[count:])).astype(BF16)
    d_input = jnp.dot(d_input, lane_flip, preferred_element_type=F32).astype(BF16)
    input_ref[...] = jnp.dot(flip[:count, :count], d_input, preferred_element_type=F32).astype(BF16)


def add_kernel(left_ref, right_ref, out_ref):
    out_ref[...] = left_ref[...] + right_ref[...]


def total_kernel(far_ref, pair_ref, from_3_or_2_ref, from_2_ref, first_ref, own_ref, out_ref):
    last = far_ref[0] == 3
    front = jnp.where(last, first_ref[...], pair_ref[...])
    out_ref[...] = front + (from_3_or_2_ref[...] + jnp.where(last, own_ref[...], from_2_ref[...]))


def spread_kernel(blocks, far_ref, gate_ref, input_ref, total_ref, whole_ref, out_ref, rows):
    count = GROUP * blocks
    got = (far_ref[0] == 1) | (far_ref[0] == 2)
    filt = jnp.where(got, whole_ref[...], total_ref[...])
    high = filt.astype(BF16).astype(F32)
    low = filt - high
    rows[pl.ds(0, count, stride=ROLES), :] = gate_ref[...].astype(F32)
    rows[pl.ds(1, count, stride=ROLES), :] = input_ref[...].astype(F32)
    for part in range(GROUP):
        at = part * blocks * ROLES
        rows[pl.ds(at + 2, blocks, stride=ROLES), :] = high
        rows[pl.ds(at + 3, blocks, stride=ROLES), :] = low
    out_ref[...] = rows[...].astype(BF16)


def unpack_kernel(far_ref, in_ref, input_ref, gate_ref, filt_ref, rows):
    chans = input_ref.shape[0]
    odd = swaps(far_ref[0]) == 1
    rows[...] = in_ref[...].astype(F32)
    gate_ref[...] = swapped(take(rows, 0, chans), odd).astype(BF16)
    input_ref[...] = swapped(take(rows, 1, chans), odd).astype(BF16)
    filt_ref[...] = swapped(take(rows, 2, chans) + take(rows, 3, chans), odd) * (1.0 / 64.0)


VMEM = pl.BlockSpec(memory_space=pltpu.VMEM)
SMEM = pl.BlockSpec(memory_space=pltpu.SMEM)


def shape(dims, dtype):
    return jax.ShapeDtypeStruct(dims, dtype)


HBM = pl.BlockSpec(memory_space=pltpu.HBM)


def in_hbm(array):
    return pltpu.with_memory_space_constraint(array, pltpu.HBM)


def call(kernel, outs, ins, scratch):
    return pl.pallas_call(
        kernel,
        out_shape=outs,
        in_specs=ins,
        out_specs=jax.tree.map(lambda _: VMEM, outs),
        scratch_shapes=scratch,
        compiler_params=pltpu.CompilerParams(vmem_limit_bytes=48 * 1024 * 1024),
    )


def swaps(group):
    return (group + 1) // 2 % 2


def send(array, *edges):
    seq = lax.axis_size("seq")
    pairs = [(i * seq + j, k * seq + (j ^ swaps(i) ^ swaps(k))) for i, k in edges for j in range(seq)]
    return lax.ppermute(array, ("far", "seq"), pairs)


def body(inputs, gate_values, grad_out, filter_raw, skip_gain):
    blocks = lax.axis_size("seq")
    far = lax.axis_index("far").reshape(1)
    chans = inputs.shape[1]
    count = GROUP * blocks
    rows = pltpu.VMEM((count * ROLES, LANES), F32)
    packed = call(
        pack_kernel,
        shape((chans * ROLES, LANES), BF16),
        [SMEM] + [HBM] * 4,
        [
            pltpu.VMEM((ROLES, chans, LANES), BF16),
            pltpu.VMEM((chans * ROLES, LANES), F32),
            pltpu.SemaphoreType.DMA((ROLES,)),
        ],
    )(far, *map(in_hbm, (inputs[0], gate_values[0], grad_out[0], filter_raw)))
    packed = lax.all_to_all(packed, ("near", "seq"), 0, 0, tiled=True)
    filt = call(
        lambda *refs: filt_kernel(blocks, *refs),
        shape((blocks, LANES), F32),
        [VMEM],
        [rows, pltpu.VMEM((2 * GROUP, 2 * blocks, LANES), F32)],
    )(packed)
    chan = lax.axis_index("near") * blocks + (lax.axis_index("seq") ^ swaps(far))
    gate, d_in, same = call(
        lambda *refs: conv_kernel(blocks, *refs),
        (shape((count, LANES), BF16), shape((count, LANES), BF16), shape((blocks, LANES), F32)),
        [SMEM, HBM, VMEM, VMEM],
        [
            rows,
            pltpu.VMEM((3 * GROUP, 2 * blocks, LANES), F32),
            pltpu.SMEM(skip_gain.shape, F32),
            pltpu.SemaphoreType.DMA(()),
        ],
    )(chan, in_hbm(skip_gain), packed, filt)
    from_2 = send(filt, (2, 0))
    from_3_or_2 = send(filt, (3, 0), (2, 3))
    from_1 = send(filt, (1, 0))
    part = shape(filt.shape, F32)
    pair = call(add_kernel, part, [VMEM] * 2, [])(same, from_1)
    first = send(pair, (0, 3))
    total = call(total_kernel, part, [SMEM] + [VMEM] * 5, [])(far, pair, from_3_or_2, from_2, first, same)
    whole = send(total, (0, 1), (3, 2))
    packed = call(
        lambda *refs: spread_kernel(blocks, *refs),
        shape((count * ROLES, LANES), BF16),
        [SMEM] + [VMEM] * 4,
        [rows],
    )(far, gate, d_in, total, whole)
    packed = lax.all_to_all(packed, ("near", "seq"), 0, 0, tiled=True)
    d_input, d_gate, d_filter = call(
        unpack_kernel,
        (shape((chans, LANES), BF16), shape((chans, LANES), BF16), shape((chans, LANES), F32)),
        [SMEM, VMEM],
        [pltpu.VMEM((chans * ROLES, LANES), F32)],
    )(far, packed)
    return d_input[None], d_gate[None], d_filter


def solution(mesh):
    sizes = mesh.devices.shape
    mesh = Mesh(mesh.devices.reshape(sizes[0] // GROUP, GROUP, sizes[1]), ("far", "near", "seq"))
    signal = P(("far", "near"), None, "seq")
    return jax.shard_map(
        body,
        mesh=mesh,
        in_specs=(signal, signal, signal, P(None, "seq"), P()),
        out_specs=(signal, signal, P(None, "seq")),
        check_vma=False,
    )
```

```python
import jax
import jax.numpy as jnp
from jax import lax
from jax.experimental import pallas as pl
from jax.experimental.pallas import tpu as pltpu
from jax.sharding import Mesh, PartitionSpec as P

LANES = 128
GROUP = 4
ROLES = 4

F32 = jnp.float32
BF16 = jnp.bfloat16


def iota(shape, dim):
    return lax.broadcasted_iota(jnp.int32, shape, dim)


def swapped(value, odd):
    up, down = jnp.roll(value, -1, axis=0), jnp.roll(value, 1, axis=0)
    other = jnp.where(iota(value.shape, 0) % 2 == 0, up, down)
    return jnp.where(odd, other, value)


def pack_kernel(far_ref, u_ref, g_ref, y_ref, k_ref, out_ref, landed, rows, sems):
    chans = out_ref.shape[0] // ROLES
    copies = [
        pltpu.make_async_copy(ref, landed.at[role], sems.at[role])
        for role, ref in enumerate((u_ref, g_ref, y_ref, k_ref))
    ]
    for copy in copies:
        copy.start()
    odd = swaps(far_ref[0]) == 1
    for role, copy in enumerate(copies):
        copy.wait()
        rows[pl.ds(role, chans, stride=ROLES), :] = swapped(landed[role].astype(F32), odd)
    out_ref[...] = rows[...].astype(BF16)


def flip_rows(count, span):
    row, col = iota((count, count), 0), iota((count, count), 1)
    same = row // span == col // span
    return jnp.where(same & (row % span + col % span == span - 1), 1.0, 0.0).astype(BF16)


def take(rows, role, count):
    return rows[pl.ds(role, count, stride=ROLES), :]


def flipped_pair(gc, flip, lane_flip):
    high = gc.astype(BF16)
    low = (gc - high.astype(F32)).astype(BF16)
    both = jnp.concatenate([high, low], axis=0)
    both = jnp.dot(both, lane_flip, preferred_element_type=F32).astype(BF16)
    return jnp.dot(flip, both, preferred_element_type=F32)


def pad(padded, value, blocks):
    for part in range(padded.shape[0]):
        padded[part, :blocks, :] = jnp.zeros((blocks, LANES), F32)
        padded[part, blocks:, :] = value[part * blocks : (part + 1) * blocks]


def shifted(padded, d, blocks):
    parts = [padded[part, blocks - d : 2 * blocks - d, :] for part in range(padded.shape[0])]
    return jnp.concatenate(parts, axis=0).astype(BF16)


def skew(value):
    return pltpu.roll(value, 0, 1, stride=1, stride_axis=0)


def filt_kernel(blocks, in_ref, filt_ref, rows, padded):
    count = GROUP * blocks
    rows[...] = in_ref[...].astype(F32)
    u = take(rows, 0, count)
    gc = take(rows, 1, count) * take(rows, 2, count)
    high = gc.astype(BF16).astype(F32)
    low = gc - high
    for part in range(2 * GROUP):
        value = high if part < GROUP else low
        at = part % GROUP * blocks
        padded[part, :blocks, :] = value[at : at + blocks]
        padded[part, blocks:, :] = jnp.zeros((blocks, LANES), F32)
    left = lax.dot_general(
        flip_rows(LANES, LANES), u.astype(BF16), (((1,), (1,)), ((), ())), preferred_element_type=F32
    ).astype(BF16)
    left = jnp.concatenate([left, left], axis=1)
    wrapped = iota((LANES, LANES), 1) <= iota((LANES, LANES), 0)
    held = None
    for pair in range(blocks // 2):
        wide = []
        for d in (2 * pair, 2 * pair + 1):
            parts = [padded[part, d : d + blocks, :] for part in range(2 * GROUP)]
            wide.append(jnp.concatenate(parts, axis=0).astype(BF16))
        products = jnp.dot(left, jnp.concatenate(wide, axis=1), preferred_element_type=F32)
        for half in range(2):
            d = 2 * pair + half
            turned = pltpu.roll(products[:, half * LANES : (half + 1) * LANES], 1, 1, stride=1, stride_axis=0)
            if held is not None:
                filt_ref[d - 1 : d, :] = jnp.sum(jnp.where(wrapped, held, turned), axis=0, keepdims=True)
            held = turned
    filt_ref[blocks - 1 : blocks, :] = jnp.sum(jnp.where(wrapped, held, 0.0), axis=0, keepdims=True)


def convolve(blocks, chan_ref, gain_ref, in_ref, gate_ref, input_ref, rows, padded, gains, sem):
    count = GROUP * blocks
    fetch = pltpu.make_async_copy(gain_ref, gains, sem)
    fetch.start()
    rows[...] = in_ref[...].astype(F32)
    u = take(rows, 0, count)
    y = take(rows, 2, count)
    gc = take(rows, 1, count) * y
    k = take(rows, 3, blocks)
    lane_flip = flip_rows(LANES, LANES)
    flip = flip_rows(2 * count, blocks)
    both = flipped_pair(gc, flip, lane_flip)
    pad(padded, jnp.concatenate([u, both], axis=0), blocks)
    inside = iota((LANES, LANES), 1) >= iota((LANES, LANES), 0)
    before = jnp.zeros((LANES, LANES), F32)
    total = jnp.zeros((3 * count, LANES), F32)
    for pair in range(blocks // 2):
        signal, toeplitz = [], []
        for d in (2 * pair, 2 * pair + 1):
            signal.append(shifted(padded, d, blocks))
            rolled = skew(jnp.broadcast_to(k[d : d + 1, :], (LANES, LANES)))
            toeplitz.append(jnp.where(inside, rolled, before).astype(BF16))
            before = rolled
        total = total + jnp.dot(
            jnp.concatenate(signal, axis=1), jnp.concatenate(toeplitz, axis=0), preferred_element_type=F32
        )
    scale = 1.0 / 64.0
    fetch.wait()
    gain = gains[chan_ref[0]]
    gate_ref[...] = (y * (total[:count] * scale + gain * u)).astype(BF16)
    corr = total[count : 2 * count] + total[2 * count :]
    d_input = (corr * scale + gain * (both[:count] + both[count:])).astype(BF16)
    d_input = jnp.dot(d_input, lane_flip, preferred_element_type=F32).astype(BF16)
    input_ref[...] = jnp.dot(flip[:count, :count], d_input, preferred_element_type=F32).astype(BF16)


def early_kernel(blocks, far_ref, chan_ref, gain_ref, in_ref, filt_ref, gate_ref, input_ref, same_ref, *scratch):
    same_ref[...] = filt_ref[...]

    @pl.when(far_ref[0] == 0)
    def _():
        convolve(blocks, chan_ref, gain_ref, in_ref, gate_ref, input_ref, *scratch)


def late_kernel(
    blocks, far_ref, chan_ref, gain_ref, in_ref, early_gate_ref, early_input_ref, after_ref, gate_ref, input_ref, *scratch
):
    @pl.when(far_ref[0] == 0)
    def _():
        gate_ref[...] = early_gate_ref[...]
        input_ref[...] = early_input_ref[...]

    @pl.when(far_ref[0] != 0)
    def _():
        convolve(blocks, chan_ref, gain_ref, in_ref, gate_ref, input_ref, *scratch)


def add_kernel(left_ref, right_ref, out_ref):
    out_ref[...] = left_ref[...] + right_ref[...]


def total_kernel(far_ref, pair_ref, from_3_or_2_ref, from_2_ref, first_ref, own_ref, out_ref):
    last = far_ref[0] == 3
    front = jnp.where(last, first_ref[...], pair_ref[...])
    out_ref[...] = front + (from_3_or_2_ref[...] + jnp.where(last, own_ref[...], from_2_ref[...]))


def spread_kernel(blocks, far_ref, gate_ref, input_ref, total_ref, whole_ref, out_ref, rows):
    count = GROUP * blocks
    got = (far_ref[0] == 1) | (far_ref[0] == 2)
    filt = jnp.where(got, whole_ref[...], total_ref[...])
    high = filt.astype(BF16).astype(F32)
    low = filt - high
    rows[pl.ds(0, count, stride=ROLES), :] = gate_ref[...].astype(F32)
    rows[pl.ds(1, count, stride=ROLES), :] = input_ref[...].astype(F32)
    for part in range(GROUP):
        at = part * blocks * ROLES
        rows[pl.ds(at + 2, blocks, stride=ROLES), :] = high
        rows[pl.ds(at + 3, blocks, stride=ROLES), :] = low
    out_ref[...] = rows[...].astype(BF16)


def unpack_kernel(far_ref, in_ref, input_ref, gate_ref, filt_ref, rows):
    chans = input_ref.shape[0]
    odd = swaps(far_ref[0]) == 1
    rows[...] = in_ref[...].astype(F32)
    gate_ref[...] = swapped(take(rows, 0, chans), odd).astype(BF16)
    input_ref[...] = swapped(take(rows, 1, chans), odd).astype(BF16)
    filt_ref[...] = swapped(take(rows, 2, chans) + take(rows, 3, chans), odd) * (1.0 / 64.0)


VMEM = pl.BlockSpec(memory_space=pltpu.VMEM)
SMEM = pl.BlockSpec(memory_space=pltpu.SMEM)


def shape(dims, dtype):
    return jax.ShapeDtypeStruct(dims, dtype)


HBM = pl.BlockSpec(memory_space=pltpu.HBM)


def in_hbm(array):
    return pltpu.with_memory_space_constraint(array, pltpu.HBM)


def call(kernel, outs, ins, scratch):
    return pl.pallas_call(
        kernel,
        out_shape=outs,
        in_specs=ins,
        out_specs=jax.tree.map(lambda _: VMEM, outs),
        scratch_shapes=scratch,
        compiler_params=pltpu.CompilerParams(vmem_limit_bytes=48 * 1024 * 1024),
    )


def swaps(group):
    return (group + 1) // 2 % 2


def send(array, *edges):
    seq = lax.axis_size("seq")
    pairs = [(i * seq + j, k * seq + (j ^ swaps(i) ^ swaps(k))) for i, k in edges for j in range(seq)]
    return lax.ppermute(array, ("far", "seq"), pairs)


def body(inputs, gate_values, grad_out, filter_raw, skip_gain):
    blocks = lax.axis_size("seq")
    far = lax.axis_index("far").reshape(1)
    chans = inputs.shape[1]
    count = GROUP * blocks
    rows = pltpu.VMEM((count * ROLES, LANES), F32)
    packed = call(
        pack_kernel,
        shape((chans * ROLES, LANES), BF16),
        [SMEM] + [HBM] * 4,
        [
            pltpu.VMEM((ROLES, chans, LANES), BF16),
            pltpu.VMEM((chans * ROLES, LANES), F32),
            pltpu.SemaphoreType.DMA((ROLES,)),
        ],
    )(far, *map(in_hbm, (inputs[0], gate_values[0], grad_out[0], filter_raw)))
    packed = lax.all_to_all(packed, ("near", "seq"), 0, 0, tiled=True)
    filt = call(
        lambda *refs: filt_kernel(blocks, *refs),
        shape((blocks, LANES), F32),
        [VMEM],
        [rows, pltpu.VMEM((2 * GROUP, 2 * blocks, LANES), F32)],
    )(packed)
    chan = lax.axis_index("near") * blocks + (lax.axis_index("seq") ^ swaps(far))
    out = shape((count, LANES), BF16)
    part = shape((blocks, LANES), F32)
    scratch = [
        rows,
        pltpu.VMEM((3 * GROUP, 2 * blocks, LANES), F32),
        pltpu.SMEM(skip_gain.shape, F32),
        pltpu.SemaphoreType.DMA(()),
    ]
    gain = in_hbm(skip_gain)
    gate, d_in, same = call(
        lambda *refs: early_kernel(blocks, *refs), (out, out, part), [SMEM, SMEM, HBM, VMEM, VMEM], scratch
    )(far, chan, gain, packed, filt)
    from_2 = send(filt, (2, 0))
    from_3_or_2 = send(filt, (3, 0), (2, 3))
    from_1 = send(filt, (1, 0))
    pair = call(add_kernel, part, [VMEM] * 2, [])(same, from_1)
    first = send(pair, (0, 3))
    total = call(total_kernel, part, [SMEM] + [VMEM] * 5, [])(far, pair, from_3_or_2, from_2, first, same)
    whole = send(total, (0, 1), (3, 2))
    gate, d_in = call(
        lambda *refs: late_kernel(blocks, *refs), (out, out), [SMEM, SMEM, HBM] + [VMEM] * 4, scratch
    )(far, chan, gain, packed, gate, d_in, total)
    packed = call(
        lambda *refs: spread_kernel(blocks, *refs),
        shape((count * ROLES, LANES), BF16),
        [SMEM] + [VMEM] * 4,
        [rows],
    )(far, gate, d_in, total, whole)
    packed = lax.all_to_all(packed, ("near", "seq"), 0, 0, tiled=True)
    d_input, d_gate, d_filter = call(
        unpack_kernel,
        (shape((chans, LANES), BF16), shape((chans, LANES), BF16), shape((chans, LANES), F32)),
        [SMEM, VMEM],
        [pltpu.VMEM((chans * ROLES, LANES), F32)],
    )(far, packed)
    return d_input[None], d_gate[None], d_filter


def solution(mesh):
    sizes = mesh.devices.shape
    mesh = Mesh(mesh.devices.reshape(sizes[0] // GROUP, GROUP, sizes[1]), ("far", "near", "seq"))
    signal = P(("far", "near"), None, "seq")
    return jax.shard_map(
        body,
        mesh=mesh,
        in_specs=(signal, signal, signal, P(None, "seq"), P()),
        out_specs=(signal, signal, P(None, "seq")),
        check_vma=False,
    )
```

```python
import jax
import jax.numpy as jnp
from jax import lax
from jax.experimental import pallas as pl
from jax.experimental.pallas import tpu as pltpu
from jax.sharding import Mesh, PartitionSpec as P

LANES = 128
GROUP = 4
ROLES = 4

F32 = jnp.float32
BF16 = jnp.bfloat16


def iota(shape, dim):
    return lax.broadcasted_iota(jnp.int32, shape, dim)


def swaps(group):
    return (group + 1) // 2 % 2


def turns(group):
    return group // 2 * (1 - group % 2)


def placed(value, group):
    up, down = jnp.roll(value, -1, axis=0), jnp.roll(value, 1, axis=0)
    value = jnp.where(swaps(group) == 1, jnp.where(iota(value.shape, 0) % 2 == 0, up, down), value)
    half = value.shape[0] // 2
    return jnp.where(turns(group) == 1, jnp.concatenate([value[half:], value[:half]], axis=0), value)


def pack_kernel(far_ref, u_ref, g_ref, y_ref, k_ref, out_ref, landed, rows, sems):
    chans = out_ref.shape[0] // ROLES
    copies = [
        pltpu.make_async_copy(ref, landed.at[role], sems.at[role])
        for role, ref in enumerate((u_ref, g_ref, y_ref, k_ref))
    ]
    for copy in copies:
        copy.start()
    for role, copy in enumerate(copies):
        copy.wait()
        rows[pl.ds(role, chans, stride=ROLES), :] = placed(landed[role].astype(F32), far_ref[0])
    out_ref[...] = rows[...].astype(BF16)


def flip_rows(count, span):
    row, col = iota((count, count), 0), iota((count, count), 1)
    same = row // span == col // span
    return jnp.where(same & (row % span + col % span == span - 1), 1.0, 0.0).astype(BF16)


def take(rows, role, count):
    return rows[pl.ds(role, count, stride=ROLES), :]


def flipped_pair(gc, flip, lane_flip):
    high = gc.astype(BF16)
    low = (gc - high.astype(F32)).astype(BF16)
    both = jnp.concatenate([high, low], axis=0)
    both = jnp.dot(both, lane_flip, preferred_element_type=F32).astype(BF16)
    return jnp.dot(flip, both, preferred_element_type=F32)


def pad(padded, value, blocks):
    for part in range(padded.shape[0]):
        padded[part, :blocks, :] = jnp.zeros((blocks, LANES), F32)
        padded[part, blocks:, :] = value[part * blocks : (part + 1) * blocks]


def shifted(padded, d, blocks):
    parts = [padded[part, blocks - d : 2 * blocks - d, :] for part in range(padded.shape[0])]
    return jnp.concatenate(parts, axis=0).astype(BF16)


def skew(value):
    return pltpu.roll(value, 0, 1, stride=1, stride_axis=0)


def filt_kernel(blocks, in_ref, filt_ref, rows, padded):
    count = GROUP * blocks
    rows[...] = in_ref[...].astype(F32)
    u = take(rows, 0, count)
    gc = take(rows, 1, count) * take(rows, 2, count)
    high = gc.astype(BF16).astype(F32)
    low = gc - high
    for part in range(2 * GROUP):
        value = high if part < GROUP else low
        at = part % GROUP * blocks
        padded[part, :blocks, :] = value[at : at + blocks]
        padded[part, blocks:, :] = jnp.zeros((blocks, LANES), F32)
    left = lax.dot_general(
        flip_rows(LANES, LANES), u.astype(BF16), (((1,), (1,)), ((), ())), preferred_element_type=F32
    ).astype(BF16)
    left = jnp.concatenate([left, left], axis=1)
    wrapped = iota((LANES, LANES), 1) <= iota((LANES, LANES), 0)
    held = None
    for pair in range(blocks // 2):
        wide = []
        for d in (2 * pair, 2 * pair + 1):
            parts = [padded[part, d : d + blocks, :] for part in range(2 * GROUP)]
            wide.append(jnp.concatenate(parts, axis=0).astype(BF16))
        products = jnp.dot(left, jnp.concatenate(wide, axis=1), preferred_element_type=F32)
        for half in range(2):
            d = 2 * pair + half
            turned = pltpu.roll(products[:, half * LANES : (half + 1) * LANES], 1, 1, stride=1, stride_axis=0)
            if held is not None:
                filt_ref[d - 1 : d, :] = jnp.sum(jnp.where(wrapped, held, turned), axis=0, keepdims=True)
            held = turned
    filt_ref[blocks - 1 : blocks, :] = jnp.sum(jnp.where(wrapped, held, 0.0), axis=0, keepdims=True)


def convolve(blocks, chan_ref, gain_ref, in_ref, gate_ref, input_ref, rows, padded, gains, sem):
    count = GROUP * blocks
    fetch = pltpu.make_async_copy(gain_ref, gains, sem)
    fetch.start()
    rows[...] = in_ref[...].astype(F32)
    u = take(rows, 0, count)
    y = take(rows, 2, count)
    gc = take(rows, 1, count) * y
    k = take(rows, 3, blocks)
    lane_flip = flip_rows(LANES, LANES)
    flip = flip_rows(2 * count, blocks)
    both = flipped_pair(gc, flip, lane_flip)
    pad(padded, jnp.concatenate([u, both], axis=0), blocks)
    inside = iota((LANES, LANES), 1) >= iota((LANES, LANES), 0)
    before = jnp.zeros((LANES, LANES), F32)
    total = jnp.zeros((3 * count, LANES), F32)
    for pair in range(blocks // 2):
        signal, toeplitz = [], []
        for d in (2 * pair, 2 * pair + 1):
            signal.append(shifted(padded, d, blocks))
            rolled = skew(jnp.broadcast_to(k[d : d + 1, :], (LANES, LANES)))
            toeplitz.append(jnp.where(inside, rolled, before).astype(BF16))
            before = rolled
        total = total + jnp.dot(
            jnp.concatenate(signal, axis=1), jnp.concatenate(toeplitz, axis=0), preferred_element_type=F32
        )
    scale = 1.0 / 64.0
    fetch.wait()
    gain = gains[chan_ref[0]]
    gate_ref[...] = (y * (total[:count] * scale + gain * u)).astype(BF16)
    corr = total[count : 2 * count] + total[2 * count :]
    d_input = (corr * scale + gain * (both[:count] + both[count:])).astype(BF16)
    d_input = jnp.dot(d_input, lane_flip, preferred_element_type=F32).astype(BF16)
    input_ref[...] = jnp.dot(flip[:count, :count], d_input, preferred_element_type=F32).astype(BF16)


def early_kernel(blocks, far_ref, chan_ref, gain_ref, in_ref, filt_ref, gate_ref, input_ref, same_ref, *scratch):
    same_ref[...] = filt_ref[...]

    @pl.when(far_ref[0] == 0)
    def _():
        convolve(blocks, chan_ref, gain_ref, in_ref, gate_ref, input_ref, *scratch)


def late_kernel(
    blocks, far_ref, chan_ref, gain_ref, in_ref, early_gate_ref, early_input_ref, after_ref, gate_ref, input_ref, *scratch
):
    @pl.when(far_ref[0] == 0)
    def _():
        gate_ref[...] = early_gate_ref[...]
        input_ref[...] = early_input_ref[...]

    @pl.when(far_ref[0] != 0)
    def _():
        convolve(blocks, chan_ref, gain_ref, in_ref, gate_ref, input_ref, *scratch)


def add_kernel(left_ref, right_ref, out_ref):
    out_ref[...] = left_ref[...] + right_ref[...]


def sum_kernel(front_ref, left_ref, right_ref, out_ref):
    out_ref[...] = front_ref[...] + (left_ref[...] + right_ref[...])


def spread_kernel(blocks, far_ref, gate_ref, input_ref, *refs):
    *sums, out_ref, rows = refs
    count = GROUP * blocks
    group = far_ref[0]
    on_0, on_1, on_2, on_3 = [ref[...] for ref in sums]
    filt = jnp.where(group < 2, jnp.where(group == 0, on_0, on_1), jnp.where(group == 2, on_2, on_3))
    high = filt.astype(BF16).astype(F32)
    low = filt - high
    rows[pl.ds(0, count, stride=ROLES), :] = gate_ref[...].astype(F32)
    rows[pl.ds(1, count, stride=ROLES), :] = input_ref[...].astype(F32)
    for part in range(GROUP):
        at = part * blocks * ROLES
        rows[pl.ds(at + 2, blocks, stride=ROLES), :] = high
        rows[pl.ds(at + 3, blocks, stride=ROLES), :] = low
    out_ref[...] = rows[...].astype(BF16)


def unpack_kernel(far_ref, in_ref, input_ref, gate_ref, filt_ref, rows):
    chans = input_ref.shape[0]
    rows[...] = in_ref[...].astype(F32)
    group = far_ref[0]
    gate_ref[...] = placed(take(rows, 0, chans), group).astype(BF16)
    input_ref[...] = placed(take(rows, 1, chans), group).astype(BF16)
    filt_ref[...] = placed(take(rows, 2, chans) + take(rows, 3, chans), group) * (1.0 / 64.0)


VMEM = pl.BlockSpec(memory_space=pltpu.VMEM)
SMEM = pl.BlockSpec(memory_space=pltpu.SMEM)


def shape(dims, dtype):
    return jax.ShapeDtypeStruct(dims, dtype)


HBM = pl.BlockSpec(memory_space=pltpu.HBM)


def in_hbm(array):
    return pltpu.with_memory_space_constraint(array, pltpu.HBM)


def call(kernel, outs, ins, scratch):
    return pl.pallas_call(
        kernel,
        out_shape=outs,
        in_specs=ins,
        out_specs=jax.tree.map(lambda _: VMEM, outs),
        scratch_shapes=scratch,
        compiler_params=pltpu.CompilerParams(vmem_limit_bytes=48 * 1024 * 1024),
    )


def send(array, *edges):
    near, seq = lax.axis_size("near"), lax.axis_size("seq")
    pairs = []
    for source, target in edges:
        turned, crossed = turns(source) ^ turns(target), swaps(source) ^ swaps(target)
        for i in range(near):
            to = (i + turned * near // 2) % near
            pairs += [((source * near + i) * seq + j, (target * near + to) * seq + (j ^ crossed)) for j in range(seq)]
    return lax.ppermute(array, ("far", "near", "seq"), pairs)


def body(inputs, gate_values, grad_out, filter_raw, skip_gain):
    blocks = lax.axis_size("seq")
    far = lax.axis_index("far").reshape(1)
    chans = inputs.shape[1]
    count = GROUP * blocks
    rows = pltpu.VMEM((count * ROLES, LANES), F32)
    packed = call(
        pack_kernel,
        shape((chans * ROLES, LANES), BF16),
        [SMEM] + [HBM] * 4,
        [
            pltpu.VMEM((ROLES, chans, LANES), BF16),
            pltpu.VMEM((chans * ROLES, LANES), F32),
            pltpu.SemaphoreType.DMA((ROLES,)),
        ],
    )(far, *map(in_hbm, (inputs[0], gate_values[0], grad_out[0], filter_raw)))
    packed = lax.all_to_all(packed, ("near", "seq"), 0, 0, tiled=True)
    filt = call(
        lambda *refs: filt_kernel(blocks, *refs),
        shape((blocks, LANES), F32),
        [VMEM],
        [rows, pltpu.VMEM((2 * GROUP, 2 * blocks, LANES), F32)],
    )(packed)
    near = lax.axis_index("near")
    near = (near + turns(far) * GROUP // 2) % GROUP
    chan = near * blocks + (lax.axis_index("seq") ^ swaps(far))
    out = shape((count, LANES), BF16)
    part = shape((blocks, LANES), F32)
    scratch = [
        rows,
        pltpu.VMEM((3 * GROUP, 2 * blocks, LANES), F32),
        pltpu.SMEM(skip_gain.shape, F32),
        pltpu.SemaphoreType.DMA(()),
    ]
    gain = in_hbm(skip_gain)
    gate, d_in, same = call(
        lambda *refs: early_kernel(blocks, *refs), (out, out, part), [SMEM, SMEM, HBM, VMEM, VMEM], scratch
    )(far, chan, gain, packed, filt)
    from_2 = send(filt, (2, 0))
    from_3_or_2 = send(filt, (3, 0), (2, 3))
    from_1 = send(filt, (1, 0))
    pair = call(add_kernel, part, [VMEM] * 2, [])(same, from_1)
    first = send(pair, (0, 3))
    total = call(sum_kernel, part, [VMEM] * 3, [])(pair, from_2, from_3_or_2)
    to_1 = send(total, (0, 1))
    total_3 = call(sum_kernel, part, [VMEM] * 3, [])(first, same, from_3_or_2)
    to_2 = send(total_3, (3, 2))
    gate, d_in = call(
        lambda *refs: late_kernel(blocks, *refs), (out, out), [SMEM, SMEM, HBM] + [VMEM] * 4, scratch
    )(far, chan, gain, packed, gate, d_in, total_3)
    packed = call(
        lambda *refs: spread_kernel(blocks, *refs),
        shape((count * ROLES, LANES), BF16),
        [SMEM] + [VMEM] * 6,
        [rows],
    )(far, gate, d_in, total, to_1, to_2, total_3)
    packed = lax.all_to_all(packed, ("near", "seq"), 0, 0, tiled=True)
    d_input, d_gate, d_filter = call(
        unpack_kernel,
        (shape((chans, LANES), BF16), shape((chans, LANES), BF16), shape((chans, LANES), F32)),
        [SMEM, VMEM],
        [pltpu.VMEM((chans * ROLES, LANES), F32)],
    )(far, packed)
    return d_input[None], d_gate[None], d_filter


def solution(mesh):
    sizes = mesh.devices.shape
    mesh = Mesh(mesh.devices.reshape(sizes[0] // GROUP, GROUP, sizes[1]), ("far", "near", "seq"))
    signal = P(("far", "near"), None, "seq")
    return jax.shard_map(
        body,
        mesh=mesh,
        in_specs=(signal, signal, signal, P(None, "seq"), P()),
        out_specs=(signal, signal, P(None, "seq")),
        check_vma=False,
    )
```

```python
import jax
import jax.numpy as jnp
from jax import lax
from jax.experimental import pallas as pl
from jax.experimental.pallas import tpu as pltpu
from jax.sharding import Mesh, PartitionSpec as P

LANES = 128
GROUP = 4
ROLES = 4

F32 = jnp.float32
BF16 = jnp.bfloat16


def iota(shape, dim):
    return lax.broadcasted_iota(jnp.int32, shape, dim)


def swaps(group):
    return (group + 3) // 4


def turns(group):
    return group // 2 * (1 - group % 2)


def placed(value, group):
    up, down = jnp.roll(value, -1, axis=0), jnp.roll(value, 1, axis=0)
    value = jnp.where(swaps(group) == 1, jnp.where(iota(value.shape, 0) % 2 == 0, up, down), value)
    half = value.shape[0] // 2
    return jnp.where(turns(group) == 1, jnp.concatenate([value[half:], value[:half]], axis=0), value)


def pack_kernel(far_ref, u_ref, g_ref, y_ref, k_ref, out_ref, landed, rows, sems):
    chans = out_ref.shape[0] // ROLES
    copies = [
        pltpu.make_async_copy(ref, landed.at[role], sems.at[role])
        for role, ref in enumerate((u_ref, g_ref, y_ref, k_ref))
    ]
    for copy in copies:
        copy.start()
    for role, copy in enumerate(copies):
        copy.wait()
        rows[pl.ds(role, chans, stride=ROLES), :] = placed(landed[role].astype(F32), far_ref[0])
    out_ref[...] = rows[...].astype(BF16)


def flip_rows(count, span):
    row, col = iota((count, count), 0), iota((count, count), 1)
    same = row // span == col // span
    return jnp.where(same & (row % span + col % span == span - 1), 1.0, 0.0).astype(BF16)


def take(rows, role, count):
    return rows[pl.ds(role, count, stride=ROLES), :]


def flipped_pair(gc, flip, lane_flip):
    high = gc.astype(BF16)
    low = (gc - high.astype(F32)).astype(BF16)
    both = jnp.concatenate([high, low], axis=0)
    both = jnp.dot(both, lane_flip, preferred_element_type=F32).astype(BF16)
    return jnp.dot(flip, both, preferred_element_type=F32)


def pad(padded, value, blocks):
    for part in range(padded.shape[0]):
        padded[part, :blocks, :] = jnp.zeros((blocks, LANES), F32)
        padded[part, blocks:, :] = value[part * blocks : (part + 1) * blocks]


def shifted(padded, d, blocks):
    parts = [padded[part, blocks - d : 2 * blocks - d, :] for part in range(padded.shape[0])]
    return jnp.concatenate(parts, axis=0).astype(BF16)


def skew(value):
    return pltpu.roll(value, 0, 1, stride=1, stride_axis=0)


def filt_kernel(blocks, in_ref, filt_ref, rows, padded):
    count = GROUP * blocks
    rows[...] = in_ref[...].astype(F32)
    u = take(rows, 0, count)
    gc = take(rows, 1, count) * take(rows, 2, count)
    high = gc.astype(BF16).astype(F32)
    low = gc - high
    for part in range(2 * GROUP):
        value = high if part < GROUP else low
        at = part % GROUP * blocks
        padded[part, :blocks, :] = value[at : at + blocks]
        padded[part, blocks:, :] = jnp.zeros((blocks, LANES), F32)
    left = lax.dot_general(
        flip_rows(LANES, LANES), u.astype(BF16), (((1,), (1,)), ((), ())), preferred_element_type=F32
    ).astype(BF16)
    left = jnp.concatenate([left, left], axis=1)
    wrapped = iota((LANES, LANES), 1) <= iota((LANES, LANES), 0)
    held = None
    for pair in range(blocks // 2):
        wide = []
        for d in (2 * pair, 2 * pair + 1):
            parts = [padded[part, d : d + blocks, :] for part in range(2 * GROUP)]
            wide.append(jnp.concatenate(parts, axis=0).astype(BF16))
        products = jnp.dot(left, jnp.concatenate(wide, axis=1), preferred_element_type=F32)
        for half in range(2):
            d = 2 * pair + half
            turned = pltpu.roll(products[:, half * LANES : (half + 1) * LANES], 1, 1, stride=1, stride_axis=0)
            if held is not None:
                filt_ref[d - 1 : d, :] = jnp.sum(jnp.where(wrapped, held, turned), axis=0, keepdims=True)
            held = turned
    filt_ref[blocks - 1 : blocks, :] = jnp.sum(jnp.where(wrapped, held, 0.0), axis=0, keepdims=True)


def convolve(blocks, chan_ref, gain_ref, in_ref, gate_ref, input_ref, rows, padded, gains, sem):
    count = GROUP * blocks
    fetch = pltpu.make_async_copy(gain_ref, gains, sem)
    fetch.start()
    rows[...] = in_ref[...].astype(F32)
    u = take(rows, 0, count)
    y = take(rows, 2, count)
    gc = take(rows, 1, count) * y
    k = take(rows, 3, blocks)
    lane_flip = flip_rows(LANES, LANES)
    flip = flip_rows(2 * count, blocks)
    both = flipped_pair(gc, flip, lane_flip)
    pad(padded, jnp.concatenate([u, both], axis=0), blocks)
    inside = iota((LANES, LANES), 1) >= iota((LANES, LANES), 0)
    before = jnp.zeros((LANES, LANES), F32)
    total = jnp.zeros((3 * count, LANES), F32)
    for pair in range(blocks // 2):
        signal, toeplitz = [], []
        for d in (2 * pair, 2 * pair + 1):
            signal.append(shifted(padded, d, blocks))
            rolled = skew(jnp.broadcast_to(k[d : d + 1, :], (LANES, LANES)))
            toeplitz.append(jnp.where(inside, rolled, before).astype(BF16))
            before = rolled
        total = total + jnp.dot(
            jnp.concatenate(signal, axis=1), jnp.concatenate(toeplitz, axis=0), preferred_element_type=F32
        )
    scale = 1.0 / 64.0
    fetch.wait()
    gain = gains[chan_ref[0]]
    gate_ref[...] = (y * (total[:count] * scale + gain * u)).astype(BF16)
    corr = total[count : 2 * count] + total[2 * count :]
    d_input = (corr * scale + gain * (both[:count] + both[count:])).astype(BF16)
    d_input = jnp.dot(d_input, lane_flip, preferred_element_type=F32).astype(BF16)
    input_ref[...] = jnp.dot(flip[:count, :count], d_input, preferred_element_type=F32).astype(BF16)


def early_kernel(blocks, far_ref, chan_ref, gain_ref, in_ref, filt_ref, gate_ref, input_ref, same_ref, *scratch):
    same_ref[...] = filt_ref[...]

    @pl.when(far_ref[0] == 0)
    def _():
        convolve(blocks, chan_ref, gain_ref, in_ref, gate_ref, input_ref, *scratch)


def late_kernel(
    blocks, far_ref, chan_ref, gain_ref, in_ref, early_gate_ref, early_input_ref, after_ref, gate_ref, input_ref, *scratch
):
    @pl.when(far_ref[0] == 0)
    def _():
        gate_ref[...] = early_gate_ref[...]
        input_ref[...] = early_input_ref[...]

    @pl.when(far_ref[0] != 0)
    def _():
        convolve(blocks, chan_ref, gain_ref, in_ref, gate_ref, input_ref, *scratch)


def add_kernel(left_ref, right_ref, out_ref):
    out_ref[...] = left_ref[...] + right_ref[...]


def last_kernel(pair_ref, own_ref, from_2_ref, after_ref, out_ref):
    out_ref[...] = (pair_ref[...] + own_ref[...]) + from_2_ref[...]


def spread_kernel(blocks, far_ref, gate_ref, input_ref, *refs):
    *sums, out_ref, rows = refs
    count = GROUP * blocks
    group = far_ref[0]
    three, from_2, early, first, on_2, on_3 = [ref[...] for ref in sums]
    on_0, on_1 = three + from_2, early + first
    filt = jnp.where(group < 2, jnp.where(group == 0, on_0, on_1), jnp.where(group == 2, on_2, on_3))
    high = filt.astype(BF16).astype(F32)
    low = filt - high
    rows[pl.ds(0, count, stride=ROLES), :] = gate_ref[...].astype(F32)
    rows[pl.ds(1, count, stride=ROLES), :] = input_ref[...].astype(F32)
    for part in range(GROUP):
        at = part * blocks * ROLES
        rows[pl.ds(at + 2, blocks, stride=ROLES), :] = high
        rows[pl.ds(at + 3, blocks, stride=ROLES), :] = low
    out_ref[...] = rows[...].astype(BF16)


def unpack_kernel(far_ref, in_ref, input_ref, gate_ref, filt_ref, rows):
    chans = input_ref.shape[0]
    rows[...] = in_ref[...].astype(F32)
    group = far_ref[0]
    gate_ref[...] = placed(take(rows, 0, chans), group).astype(BF16)
    input_ref[...] = placed(take(rows, 1, chans), group).astype(BF16)
    filt_ref[...] = placed(take(rows, 2, chans) + take(rows, 3, chans), group) * (1.0 / 64.0)


VMEM = pl.BlockSpec(memory_space=pltpu.VMEM)
SMEM = pl.BlockSpec(memory_space=pltpu.SMEM)


def shape(dims, dtype):
    return jax.ShapeDtypeStruct(dims, dtype)


HBM = pl.BlockSpec(memory_space=pltpu.HBM)


def in_hbm(array):
    return pltpu.with_memory_space_constraint(array, pltpu.HBM)


def call(kernel, outs, ins, scratch):
    return pl.pallas_call(
        kernel,
        out_shape=outs,
        in_specs=ins,
        out_specs=jax.tree.map(lambda _: VMEM, outs),
        scratch_shapes=scratch,
        compiler_params=pltpu.CompilerParams(vmem_limit_bytes=48 * 1024 * 1024),
    )


def send(array, *edges):
    near, seq = lax.axis_size("near"), lax.axis_size("seq")
    pairs = []
    for source, target in edges:
        turned, crossed = turns(source) ^ turns(target), swaps(source) ^ swaps(target)
        for i in range(near):
            to = (i + turned * near // 2) % near
            pairs += [((source * near + i) * seq + j, (target * near + to) * seq + (j ^ crossed)) for j in range(seq)]
    return lax.ppermute(array, ("far", "near", "seq"), pairs)


def body(inputs, gate_values, grad_out, filter_raw, skip_gain):
    blocks = lax.axis_size("seq")
    far = lax.axis_index("far").reshape(1)
    chans = inputs.shape[1]
    count = GROUP * blocks
    rows = pltpu.VMEM((count * ROLES, LANES), F32)
    packed = call(
        pack_kernel,
        shape((chans * ROLES, LANES), BF16),
        [SMEM] + [HBM] * 4,
        [
            pltpu.VMEM((ROLES, chans, LANES), BF16),
            pltpu.VMEM((chans * ROLES, LANES), F32),
            pltpu.SemaphoreType.DMA((ROLES,)),
        ],
    )(far, *map(in_hbm, (inputs[0], gate_values[0], grad_out[0], filter_raw)))
    packed = lax.all_to_all(packed, ("near", "seq"), 0, 0, tiled=True)
    filt = call(
        lambda *refs: filt_kernel(blocks, *refs),
        shape((blocks, LANES), F32),
        [VMEM],
        [rows, pltpu.VMEM((2 * GROUP, 2 * blocks, LANES), F32)],
    )(packed)
    near = lax.axis_index("near")
    near = (near + turns(far) * GROUP // 2) % GROUP
    chan = near * blocks + (lax.axis_index("seq") ^ swaps(far))
    out = shape((count, LANES), BF16)
    part = shape((blocks, LANES), F32)
    scratch = [
        rows,
        pltpu.VMEM((3 * GROUP, 2 * blocks, LANES), F32),
        pltpu.SMEM(skip_gain.shape, F32),
        pltpu.SemaphoreType.DMA(()),
    ]
    gain = in_hbm(skip_gain)
    gate, d_in, same = call(
        lambda *refs: early_kernel(blocks, *refs), (out, out, part), [SMEM, SMEM, HBM, VMEM, VMEM], scratch
    )(far, chan, gain, packed, filt)
    from_2 = send(filt, (2, 0))
    from_3_or_2 = send(filt, (3, 0), (2, 3))
    from_1 = send(filt, (1, 0))
    pair = call(add_kernel, part, [VMEM] * 2, [])(same, from_1)
    first = send(pair, (0, 3), (2, 1))
    three = call(add_kernel, part, [VMEM] * 2, [])(pair, from_3_or_2)
    early = send(three, (0, 1))
    total_3 = call(last_kernel, part, [VMEM] * 4, [])(first, same, from_3_or_2, from_2)
    to_2 = send(total_3, (3, 2))
    gate, d_in = call(
        lambda *refs: late_kernel(blocks, *refs), (out, out), [SMEM, SMEM, HBM] + [VMEM] * 4, scratch
    )(far, chan, gain, packed, gate, d_in, three)
    packed = call(
        lambda *refs: spread_kernel(blocks, *refs),
        shape((count * ROLES, LANES), BF16),
        [SMEM] + [VMEM] * 8,
        [rows],
    )(far, gate, d_in, three, from_2, early, first, to_2, total_3)
    packed = lax.all_to_all(packed, ("near", "seq"), 0, 0, tiled=True)
    d_input, d_gate, d_filter = call(
        unpack_kernel,
        (shape((chans, LANES), BF16), shape((chans, LANES), BF16), shape((chans, LANES), F32)),
        [SMEM, VMEM],
        [pltpu.VMEM((chans * ROLES, LANES), F32)],
    )(far, packed)
    return d_input[None], d_gate[None], d_filter


def solution(mesh):
    sizes = mesh.devices.shape
    mesh = Mesh(mesh.devices.reshape(sizes[0] // GROUP, GROUP, sizes[1]), ("far", "near", "seq"))
    signal = P(("far", "near"), None, "seq")
    return jax.shard_map(
        body,
        mesh=mesh,
        in_specs=(signal, signal, signal, P(None, "seq"), P()),
        out_specs=(signal, signal, P(None, "seq")),
        check_vma=False,
    )
```

```python
import jax
import jax.numpy as jnp
from jax import lax
from jax.experimental import pallas as pl
from jax.experimental.pallas import tpu as pltpu
from jax.sharding import Mesh, PartitionSpec as P

LANES = 128
GROUP = 4
ROLES = 4

F32 = jnp.float32
BF16 = jnp.bfloat16


def iota(shape, dim):
    return lax.broadcasted_iota(jnp.int32, shape, dim)


def swaps(group):
    return group // 2 * (1 - group % 2)


def turns(group):
    return group // 2 * (1 - group % 2)


def placed(value, group):
    up, down = jnp.roll(value, -1, axis=0), jnp.roll(value, 1, axis=0)
    value = jnp.where(swaps(group) == 1, jnp.where(iota(value.shape, 0) % 2 == 0, up, down), value)
    half = value.shape[0] // 2
    return jnp.where(turns(group) == 1, jnp.concatenate([value[half:], value[:half]], axis=0), value)


def pack_kernel(far_ref, u_ref, g_ref, y_ref, k_ref, out_ref, landed, rows, sems):
    chans = out_ref.shape[0] // ROLES
    copies = [
        pltpu.make_async_copy(ref, landed.at[role], sems.at[role])
        for role, ref in enumerate((u_ref, g_ref, y_ref, k_ref))
    ]
    for copy in copies:
        copy.start()
    for role, copy in enumerate(copies):
        copy.wait()
        rows[pl.ds(role, chans, stride=ROLES), :] = placed(landed[role].astype(F32), far_ref[0])
    out_ref[...] = rows[...].astype(BF16)


def flip_rows(count, span):
    row, col = iota((count, count), 0), iota((count, count), 1)
    same = row // span == col // span
    return jnp.where(same & (row % span + col % span == span - 1), 1.0, 0.0).astype(BF16)


def take(rows, role, count):
    return rows[pl.ds(role, count, stride=ROLES), :]


def flipped_pair(gc, flip, lane_flip):
    high = gc.astype(BF16)
    low = (gc - high.astype(F32)).astype(BF16)
    both = jnp.concatenate([high, low], axis=0)
    both = jnp.dot(both, lane_flip, preferred_element_type=F32).astype(BF16)
    return jnp.dot(flip, both, preferred_element_type=F32)


def pad(padded, value, blocks):
    for part in range(padded.shape[0]):
        padded[part, :blocks, :] = jnp.zeros((blocks, LANES), F32)
        padded[part, blocks:, :] = value[part * blocks : (part + 1) * blocks]


def shifted(padded, d, blocks):
    parts = [padded[part, blocks - d : 2 * blocks - d, :] for part in range(padded.shape[0])]
    return jnp.concatenate(parts, axis=0).astype(BF16)


def skew(value):
    return pltpu.roll(value, 0, 1, stride=1, stride_axis=0)


def filt_kernel(blocks, in_ref, filt_ref, rows, padded):
    count = GROUP * blocks
    rows[...] = in_ref[...].astype(F32)
    u = take(rows, 0, count)
    gc = take(rows, 1, count) * take(rows, 2, count)
    high = gc.astype(BF16).astype(F32)
    low = gc - high
    for part in range(2 * GROUP):
        value = high if part < GROUP else low
        at = part % GROUP * blocks
        padded[part, :blocks, :] = value[at : at + blocks]
        padded[part, blocks:, :] = jnp.zeros((blocks, LANES), F32)
    left = lax.dot_general(
        flip_rows(LANES, LANES), u.astype(BF16), (((1,), (1,)), ((), ())), preferred_element_type=F32
    ).astype(BF16)
    left = jnp.concatenate([left, left], axis=1)
    wrapped = iota((LANES, LANES), 1) <= iota((LANES, LANES), 0)
    held = None
    for pair in range(blocks // 2):
        wide = []
        for d in (2 * pair, 2 * pair + 1):
            parts = [padded[part, d : d + blocks, :] for part in range(2 * GROUP)]
            wide.append(jnp.concatenate(parts, axis=0).astype(BF16))
        products = jnp.dot(left, jnp.concatenate(wide, axis=1), preferred_element_type=F32)
        for half in range(2):
            d = 2 * pair + half
            turned = pltpu.roll(products[:, half * LANES : (half + 1) * LANES], 1, 1, stride=1, stride_axis=0)
            if held is not None:
                filt_ref[d - 1 : d, :] = jnp.sum(jnp.where(wrapped, held, turned), axis=0, keepdims=True)
            held = turned
    filt_ref[blocks - 1 : blocks, :] = jnp.sum(jnp.where(wrapped, held, 0.0), axis=0, keepdims=True)


def convolve(blocks, chan_ref, gain_ref, in_ref, gate_ref, input_ref, rows, padded, gains, sem):
    count = GROUP * blocks
    fetch = pltpu.make_async_copy(gain_ref, gains, sem)
    fetch.start()
    rows[...] = in_ref[...].astype(F32)
    u = take(rows, 0, count)
    y = take(rows, 2, count)
    gc = take(rows, 1, count) * y
    k = take(rows, 3, blocks)
    lane_flip = flip_rows(LANES, LANES)
    flip = flip_rows(2 * count, blocks)
    both = flipped_pair(gc, flip, lane_flip)
    pad(padded, jnp.concatenate([u, both], axis=0), blocks)
    inside = iota((LANES, LANES), 1) >= iota((LANES, LANES), 0)
    before = jnp.zeros((LANES, LANES), F32)
    total = jnp.zeros((3 * count, LANES), F32)
    for pair in range(blocks // 2):
        signal, toeplitz = [], []
        for d in (2 * pair, 2 * pair + 1):
            signal.append(shifted(padded, d, blocks))
            rolled = skew(jnp.broadcast_to(k[d : d + 1, :], (LANES, LANES)))
            toeplitz.append(jnp.where(inside, rolled, before).astype(BF16))
            before = rolled
        total = total + jnp.dot(
            jnp.concatenate(signal, axis=1), jnp.concatenate(toeplitz, axis=0), preferred_element_type=F32
        )
    scale = 1.0 / 64.0
    fetch.wait()
    gain = gains[chan_ref[0]]
    gate_ref[...] = (y * (total[:count] * scale + gain * u)).astype(BF16)
    corr = total[count : 2 * count] + total[2 * count :]
    d_input = (corr * scale + gain * (both[:count] + both[count:])).astype(BF16)
    d_input = jnp.dot(d_input, lane_flip, preferred_element_type=F32).astype(BF16)
    input_ref[...] = jnp.dot(flip[:count, :count], d_input, preferred_element_type=F32).astype(BF16)


def early_kernel(blocks, far_ref, chan_ref, gain_ref, in_ref, filt_ref, gate_ref, input_ref, same_ref, *scratch):
    same_ref[...] = filt_ref[...]

    @pl.when(far_ref[0] == 0)
    def _():
        convolve(blocks, chan_ref, gain_ref, in_ref, gate_ref, input_ref, *scratch)


def late_kernel(
    blocks, far_ref, chan_ref, gain_ref, in_ref, early_gate_ref, early_input_ref, after_ref, gate_ref, input_ref, *scratch
):
    @pl.when(far_ref[0] == 0)
    def _():
        gate_ref[...] = early_gate_ref[...]
        input_ref[...] = early_input_ref[...]

    @pl.when(far_ref[0] != 0)
    def _():
        convolve(blocks, chan_ref, gain_ref, in_ref, gate_ref, input_ref, *scratch)


def add_kernel(left_ref, right_ref, out_ref):
    out_ref[...] = left_ref[...] + right_ref[...]


def last_kernel(pair_ref, own_ref, after_ref, out_ref):
    out_ref[...] = pair_ref[...] + own_ref[...]


def spread_kernel(blocks, far_ref, gate_ref, input_ref, *refs):
    *sums, out_ref, rows = refs
    count = GROUP * blocks
    group = far_ref[0]
    own, from_2, three, early, first, three_3, to_2 = [ref[...] for ref in sums]
    on_0, on_1, on_2, on_3 = three + from_2, early + first, to_2 + own, three_3 + early
    filt = jnp.where(group < 2, jnp.where(group == 0, on_0, on_1), jnp.where(group == 2, on_2, on_3))
    high = filt.astype(BF16).astype(F32)
    low = filt - high
    rows[pl.ds(0, count, stride=ROLES), :] = gate_ref[...].astype(F32)
    rows[pl.ds(1, count, stride=ROLES), :] = input_ref[...].astype(F32)
    for part in range(GROUP):
        at = part * blocks * ROLES
        rows[pl.ds(at + 2, blocks, stride=ROLES), :] = high
        rows[pl.ds(at + 3, blocks, stride=ROLES), :] = low
    out_ref[...] = rows[...].astype(BF16)


def unpack_kernel(far_ref, in_ref, input_ref, gate_ref, filt_ref, rows):
    chans = input_ref.shape[0]
    rows[...] = in_ref[...].astype(F32)
    group = far_ref[0]
    gate_ref[...] = placed(take(rows, 0, chans), group).astype(BF16)
    input_ref[...] = placed(take(rows, 1, chans), group).astype(BF16)
    filt_ref[...] = placed(take(rows, 2, chans) + take(rows, 3, chans), group) * (1.0 / 64.0)


VMEM = pl.BlockSpec(memory_space=pltpu.VMEM)
SMEM = pl.BlockSpec(memory_space=pltpu.SMEM)


def shape(dims, dtype):
    return jax.ShapeDtypeStruct(dims, dtype)


HBM = pl.BlockSpec(memory_space=pltpu.HBM)


def in_hbm(array):
    return pltpu.with_memory_space_constraint(array, pltpu.HBM)


def call(kernel, outs, ins, scratch):
    return pl.pallas_call(
        kernel,
        out_shape=outs,
        in_specs=ins,
        out_specs=jax.tree.map(lambda _: VMEM, outs),
        scratch_shapes=scratch,
        compiler_params=pltpu.CompilerParams(vmem_limit_bytes=48 * 1024 * 1024),
    )


def send(array, *edges):
    near, seq = lax.axis_size("near"), lax.axis_size("seq")
    pairs = []
    for source, target in edges:
        turned, crossed = turns(source) ^ turns(target), swaps(source) ^ swaps(target)
        for i in range(near):
            to = (i + turned * near // 2) % near
            pairs += [((source * near + i) * seq + j, (target * near + to) * seq + (j ^ crossed)) for j in range(seq)]
    return lax.ppermute(array, ("far", "near", "seq"), pairs)


def body(inputs, gate_values, grad_out, filter_raw, skip_gain):
    blocks = lax.axis_size("seq")
    far = lax.axis_index("far").reshape(1)
    chans = inputs.shape[1]
    count = GROUP * blocks
    rows = pltpu.VMEM((count * ROLES, LANES), F32)
    packed = call(
        pack_kernel,
        shape((chans * ROLES, LANES), BF16),
        [SMEM] + [HBM] * 4,
        [
            pltpu.VMEM((ROLES, chans, LANES), BF16),
            pltpu.VMEM((chans * ROLES, LANES), F32),
            pltpu.SemaphoreType.DMA((ROLES,)),
        ],
    )(far, *map(in_hbm, (inputs[0], gate_values[0], grad_out[0], filter_raw)))
    packed = lax.all_to_all(packed, ("near", "seq"), 0, 0, tiled=True)
    filt = call(
        lambda *refs: filt_kernel(blocks, *refs),
        shape((blocks, LANES), F32),
        [VMEM],
        [rows, pltpu.VMEM((2 * GROUP, 2 * blocks, LANES), F32)],
    )(packed)
    near = lax.axis_index("near")
    near = (near + turns(far) * GROUP // 2) % GROUP
    chan = near * blocks + (lax.axis_index("seq") ^ swaps(far))
    out = shape((count, LANES), BF16)
    part = shape((blocks, LANES), F32)
    scratch = [
        rows,
        pltpu.VMEM((3 * GROUP, 2 * blocks, LANES), F32),
        pltpu.SMEM(skip_gain.shape, F32),
        pltpu.SemaphoreType.DMA(()),
    ]
    gain = in_hbm(skip_gain)
    gate, d_in, same = call(
        lambda *refs: early_kernel(blocks, *refs), (out, out, part), [SMEM, SMEM, HBM, VMEM, VMEM], scratch
    )(far, chan, gain, packed, filt)
    from_2 = send(filt, (2, 0))
    from_3 = send(filt, (3, 0))
    from_1 = send(filt, (1, 0))
    pair = call(add_kernel, part, [VMEM] * 2, [])(same, from_1)
    first = send(pair, (0, 3), (2, 1))
    three = call(add_kernel, part, [VMEM] * 2, [])(pair, from_3)
    early = send(three, (0, 1), (2, 3))
    three_3 = call(last_kernel, part, [VMEM] * 3, [])(first, same, from_2)
    to_2 = send(three_3, (3, 2))
    gate, d_in = call(
        lambda *refs: late_kernel(blocks, *refs), (out, out), [SMEM, SMEM, HBM] + [VMEM] * 4, scratch
    )(far, chan, gain, packed, gate, d_in, three)
    packed = call(
        lambda *refs: spread_kernel(blocks, *refs),
        shape((count * ROLES, LANES), BF16),
        [SMEM] + [VMEM] * 9,
        [rows],
    )(far, gate, d_in, same, from_2, three, early, first, three_3, to_2)
    packed = lax.all_to_all(packed, ("near", "seq"), 0, 0, tiled=True)
    d_input, d_gate, d_filter = call(
        unpack_kernel,
        (shape((chans, LANES), BF16), shape((chans, LANES), BF16), shape((chans, LANES), F32)),
        [SMEM, VMEM],
        [pltpu.VMEM((chans * ROLES, LANES), F32)],
    )(far, packed)
    return d_input[None], d_gate[None], d_filter


def solution(mesh):
    sizes = mesh.devices.shape
    mesh = Mesh(mesh.devices.reshape(sizes[0] // GROUP, GROUP, sizes[1]), ("far", "near", "seq"))
    signal = P(("far", "near"), None, "seq")
    return jax.shard_map(
        body,
        mesh=mesh,
        in_specs=(signal, signal, signal, P(None, "seq"), P()),
        out_specs=(signal, signal, P(None, "seq")),
        check_vma=False,
    )
```

```python
import jax
import jax.numpy as jnp
from jax import lax
from jax.experimental import pallas as pl
from jax.experimental.pallas import tpu as pltpu
from jax.sharding import Mesh, PartitionSpec as P

LANES = 128
GROUP = 4
ROLES = 4

F32 = jnp.float32
BF16 = jnp.bfloat16


def iota(shape, dim):
    return lax.broadcasted_iota(jnp.int32, shape, dim)


def swaps(group):
    return group % 2


def turns(group):
    return group // 2 * (1 - group % 2)


def by_group(group, plain, swapped, turned):
    pl.when(group == 0)(plain)
    pl.when(swaps(group) == 1)(swapped)
    pl.when(turns(group) == 1)(turned)


def neighbours(value):
    up, down = jnp.roll(value, -1, axis=0), jnp.roll(value, 1, axis=0)
    return jnp.where(iota(value.shape, 0) % 2 == 0, up, down)


def halves(value):
    half = value.shape[0] // 2
    return jnp.concatenate([value[half:], value[:half]], axis=0)


def pack_kernel(far_ref, u_ref, g_ref, y_ref, k_ref, out_ref, landed, rows, sems):
    chans = out_ref.shape[0] // ROLES
    copies = [
        pltpu.make_async_copy(ref, landed.at[role], sems.at[role])
        for role, ref in enumerate((u_ref, g_ref, y_ref, k_ref))
    ]
    for copy in copies:
        copy.start()
    for copy in copies:
        copy.wait()

    def store(order):
        for role in range(ROLES):
            rows[pl.ds(role, chans, stride=ROLES), :] = order(landed[role].astype(F32))
        out_ref[...] = rows[...].astype(BF16)

    by_group(far_ref[0], lambda: store(lambda value: value), lambda: store(neighbours), lambda: store(halves))


def flip_rows(count, span):
    row, col = iota((count, count), 0), iota((count, count), 1)
    same = row // span == col // span
    return jnp.where(same & (row % span + col % span == span - 1), 1.0, 0.0).astype(BF16)


def take(rows, role, count):
    return rows[pl.ds(role, count, stride=ROLES), :]


def flipped_pair(gc, flip, lane_flip):
    high = gc.astype(BF16)
    low = (gc - high.astype(F32)).astype(BF16)
    both = jnp.concatenate([high, low], axis=0)
    both = jnp.dot(both, lane_flip, preferred_element_type=F32).astype(BF16)
    return jnp.dot(flip, both, preferred_element_type=F32)


def pad(padded, value, blocks):
    for part in range(padded.shape[0]):
        padded[part, :blocks, :] = jnp.zeros((blocks, LANES), F32)
        padded[part, blocks:, :] = value[part * blocks : (part + 1) * blocks]


def shifted(padded, d, blocks):
    parts = [padded[part, blocks - d : 2 * blocks - d, :] for part in range(padded.shape[0])]
    return jnp.concatenate(parts, axis=0).astype(BF16)


def skew(value):
    return pltpu.roll(value, 0, 1, stride=1, stride_axis=0)


def filt_kernel(blocks, in_ref, filt_ref, rows, padded):
    count = GROUP * blocks
    rows[...] = in_ref[...].astype(F32)
    u = take(rows, 0, count)
    gc = take(rows, 1, count) * take(rows, 2, count)
    high = gc.astype(BF16).astype(F32)
    low = gc - high
    for part in range(2 * GROUP):
        value = high if part < GROUP else low
        at = part % GROUP * blocks
        padded[part, :blocks, :] = value[at : at + blocks]
        padded[part, blocks:, :] = jnp.zeros((blocks, LANES), F32)
    left = lax.dot_general(
        flip_rows(LANES, LANES), u.astype(BF16), (((1,), (1,)), ((), ())), preferred_element_type=F32
    ).astype(BF16)
    left = jnp.concatenate([left, left], axis=1)
    wrapped = iota((LANES, LANES), 1) <= iota((LANES, LANES), 0)
    held = None
    for pair in range(blocks // 2):
        wide = []
        for d in (2 * pair, 2 * pair + 1):
            parts = [padded[part, d : d + blocks, :] for part in range(2 * GROUP)]
            wide.append(jnp.concatenate(parts, axis=0).astype(BF16))
        products = jnp.dot(left, jnp.concatenate(wide, axis=1), preferred_element_type=F32)
        for half in range(2):
            d = 2 * pair + half
            turned = pltpu.roll(products[:, half * LANES : (half + 1) * LANES], 1, 1, stride=1, stride_axis=0)
            if held is not None:
                filt_ref[d - 1 : d, :] = jnp.sum(jnp.where(wrapped, held, turned), axis=0, keepdims=True)
            held = turned
    filt_ref[blocks - 1 : blocks, :] = jnp.sum(jnp.where(wrapped, held, 0.0), axis=0, keepdims=True)


def convolve(blocks, chan_ref, gain_ref, in_ref, gate_ref, input_ref, rows, padded, gains, sem):
    count = GROUP * blocks
    fetch = pltpu.make_async_copy(gain_ref, gains, sem)
    fetch.start()
    rows[...] = in_ref[...].astype(F32)
    u = take(rows, 0, count)
    y = take(rows, 2, count)
    gc = take(rows, 1, count) * y
    k = take(rows, 3, blocks)
    lane_flip = flip_rows(LANES, LANES)
    flip = flip_rows(2 * count, blocks)
    both = flipped_pair(gc, flip, lane_flip)
    pad(padded, jnp.concatenate([u, both], axis=0), blocks)
    inside = iota((LANES, LANES), 1) >= iota((LANES, LANES), 0)
    before = jnp.zeros((LANES, LANES), F32)
    total = jnp.zeros((3 * count, LANES), F32)
    for pair in range(blocks // 2):
        signal, toeplitz = [], []
        for d in (2 * pair, 2 * pair + 1):
            signal.append(shifted(padded, d, blocks))
            rolled = skew(jnp.broadcast_to(k[d : d + 1, :], (LANES, LANES)))
            toeplitz.append(jnp.where(inside, rolled, before).astype(BF16))
            before = rolled
        total = total + jnp.dot(
            jnp.concatenate(signal, axis=1), jnp.concatenate(toeplitz, axis=0), preferred_element_type=F32
        )
    scale = 1.0 / 64.0
    fetch.wait()
    gain = gains[chan_ref[0]]
    gate_ref[...] = (y * (total[:count] * scale + gain * u)).astype(BF16)
    corr = total[count : 2 * count] + total[2 * count :]
    d_input = (corr * scale + gain * (both[:count] + both[count:])).astype(BF16)
    d_input = jnp.dot(d_input, lane_flip, preferred_element_type=F32).astype(BF16)
    input_ref[...] = jnp.dot(flip[:count, :count], d_input, preferred_element_type=F32).astype(BF16)


def early_kernel(blocks, far_ref, chan_ref, gain_ref, in_ref, filt_ref, gate_ref, input_ref, same_ref, *scratch):
    same_ref[...] = filt_ref[...]

    @pl.when(far_ref[0] == 0)
    def _():
        convolve(blocks, chan_ref, gain_ref, in_ref, gate_ref, input_ref, *scratch)


def late_kernel(
    blocks, far_ref, chan_ref, gain_ref, in_ref, early_gate_ref, early_input_ref, after_ref, gate_ref, input_ref, *scratch
):
    @pl.when(far_ref[0] == 0)
    def _():
        gate_ref[...] = early_gate_ref[...]
        input_ref[...] = early_input_ref[...]

    @pl.when(far_ref[0] != 0)
    def _():
        convolve(blocks, chan_ref, gain_ref, in_ref, gate_ref, input_ref, *scratch)


def add_kernel(left_ref, right_ref, out_ref):
    out_ref[...] = left_ref[...] + right_ref[...]


def last_kernel(pair_ref, own_ref, after_ref, out_ref):
    out_ref[...] = pair_ref[...] + own_ref[...]


def spread_kernel(blocks, far_ref, gate_ref, input_ref, *refs):
    *sums, out_ref, rows = refs
    count = GROUP * blocks
    group = far_ref[0]
    own, from_2, three, early, first, three_3, to_2 = [ref[...] for ref in sums]
    on_0, on_1, on_2, on_3 = three + from_2, early + first, to_2 + own, three_3 + early
    filt = jnp.where(group < 2, jnp.where(group == 0, on_0, on_1), jnp.where(group == 2, on_2, on_3))
    high = filt.astype(BF16).astype(F32)
    low = filt - high
    rows[pl.ds(0, count, stride=ROLES), :] = gate_ref[...].astype(F32)
    rows[pl.ds(1, count, stride=ROLES), :] = input_ref[...].astype(F32)
    for part in range(GROUP):
        at = part * blocks * ROLES
        rows[pl.ds(at + 2, blocks, stride=ROLES), :] = high
        rows[pl.ds(at + 3, blocks, stride=ROLES), :] = low
    out_ref[...] = rows[...].astype(BF16)


def unpack_kernel(far_ref, in_ref, input_ref, gate_ref, filt_ref, rows):
    chans = input_ref.shape[0]
    rows[...] = in_ref[...].astype(F32)

    def store(order):
        gate_ref[...] = order(take(rows, 0, chans)).astype(BF16)
        input_ref[...] = order(take(rows, 1, chans)).astype(BF16)
        filt_ref[...] = order(take(rows, 2, chans) + take(rows, 3, chans)) * (1.0 / 64.0)

    by_group(far_ref[0], lambda: store(lambda value: value), lambda: store(neighbours), lambda: store(halves))


VMEM = pl.BlockSpec(memory_space=pltpu.VMEM)
SMEM = pl.BlockSpec(memory_space=pltpu.SMEM)


def shape(dims, dtype):
    return jax.ShapeDtypeStruct(dims, dtype)


HBM = pl.BlockSpec(memory_space=pltpu.HBM)


def in_hbm(array):
    return pltpu.with_memory_space_constraint(array, pltpu.HBM)


def call(kernel, outs, ins, scratch):
    return pl.pallas_call(
        kernel,
        out_shape=outs,
        in_specs=ins,
        out_specs=jax.tree.map(lambda _: VMEM, outs),
        scratch_shapes=scratch,
        compiler_params=pltpu.CompilerParams(vmem_limit_bytes=48 * 1024 * 1024),
    )


def send(array, *edges):
    near, seq = lax.axis_size("near"), lax.axis_size("seq")
    pairs = []
    for source, target in edges:
        turned, crossed = turns(source) ^ turns(target), swaps(source) ^ swaps(target)
        for i in range(near):
            to = (i + turned * near // 2) % near
            pairs += [((source * near + i) * seq + j, (target * near + to) * seq + (j ^ crossed)) for j in range(seq)]
    return lax.ppermute(array, ("far", "near", "seq"), pairs)


def body(inputs, gate_values, grad_out, filter_raw, skip_gain):
    blocks = lax.axis_size("seq")
    far = lax.axis_index("far").reshape(1)
    chans = inputs.shape[1]
    count = GROUP * blocks
    rows = pltpu.VMEM((count * ROLES, LANES), F32)
    packed = call(
        pack_kernel,
        shape((chans * ROLES, LANES), BF16),
        [SMEM] + [HBM] * 4,
        [
            pltpu.VMEM((ROLES, chans, LANES), BF16),
            pltpu.VMEM((chans * ROLES, LANES), F32),
            pltpu.SemaphoreType.DMA((ROLES,)),
        ],
    )(far, *map(in_hbm, (inputs[0], gate_values[0], grad_out[0], filter_raw)))
    packed = lax.all_to_all(packed, ("near", "seq"), 0, 0, tiled=True)
    filt = call(
        lambda *refs: filt_kernel(blocks, *refs),
        shape((blocks, LANES), F32),
        [VMEM],
        [rows, pltpu.VMEM((2 * GROUP, 2 * blocks, LANES), F32)],
    )(packed)
    near = lax.axis_index("near")
    near = (near + turns(far) * GROUP // 2) % GROUP
    chan = near * blocks + (lax.axis_index("seq") ^ swaps(far))
    out = shape((count, LANES), BF16)
    part = shape((blocks, LANES), F32)
    scratch = [
        rows,
        pltpu.VMEM((3 * GROUP, 2 * blocks, LANES), F32),
        pltpu.SMEM(skip_gain.shape, F32),
        pltpu.SemaphoreType.DMA(()),
    ]
    gain = in_hbm(skip_gain)
    gate, d_in, same = call(
        lambda *refs: early_kernel(blocks, *refs), (out, out, part), [SMEM, SMEM, HBM, VMEM, VMEM], scratch
    )(far, chan, gain, packed, filt)
    from_2 = send(filt, (2, 0))
    from_3 = send(filt, (3, 0))
    from_1 = send(filt, (1, 0))
    pair = call(add_kernel, part, [VMEM] * 2, [])(same, from_1)
    first = send(pair, (0, 3), (2, 1))
    three = call(add_kernel, part, [VMEM] * 2, [])(pair, from_3)
    early = send(three, (0, 1), (2, 3))
    three_3 = call(last_kernel, part, [VMEM] * 3, [])(first, same, from_2)
    to_2 = send(three_3, (3, 2))
    gate, d_in = call(
        lambda *refs: late_kernel(blocks, *refs), (out, out), [SMEM, SMEM, HBM] + [VMEM] * 4, scratch
    )(far, chan, gain, packed, gate, d_in, three)
    packed = call(
        lambda *refs: spread_kernel(blocks, *refs),
        shape((count * ROLES, LANES), BF16),
        [SMEM] + [VMEM] * 9,
        [rows],
    )(far, gate, d_in, same, from_2, three, early, first, three_3, to_2)
    packed = lax.all_to_all(packed, ("near", "seq"), 0, 0, tiled=True)
    d_input, d_gate, d_filter = call(
        unpack_kernel,
        (shape((chans, LANES), BF16), shape((chans, LANES), BF16), shape((chans, LANES), F32)),
        [SMEM, VMEM],
        [pltpu.VMEM((chans * ROLES, LANES), F32)],
    )(far, packed)
    return d_input[None], d_gate[None], d_filter


def solution(mesh):
    sizes = mesh.devices.shape
    mesh = Mesh(mesh.devices.reshape(sizes[0] // GROUP, GROUP, sizes[1]), ("far", "near", "seq"))
    signal = P(("far", "near"), None, "seq")
    return jax.shard_map(
        body,
        mesh=mesh,
        in_specs=(signal, signal, signal, P(None, "seq"), P()),
        out_specs=(signal, signal, P(None, "seq")),
        check_vma=False,
    )
```

```python
import jax
import jax.numpy as jnp
from jax import lax
from jax.experimental import pallas as pl
from jax.experimental.pallas import tpu as pltpu
from jax.sharding import Mesh, PartitionSpec as P

LANES = 128
GROUP = 4
ROLES = 4

F32 = jnp.float32
BF16 = jnp.bfloat16


def iota(shape, dim):
    return lax.broadcasted_iota(jnp.int32, shape, dim)


def swaps(group):
    return group % 2


HELD = (1, 3, 0, 2)
HOLDER = (2, 0, 3, 1)


def turns(group):
    return group // 2 * (1 - group % 2)


def by_group(group, plain, swapped, turned):
    pl.when(group == 0)(plain)
    pl.when(swaps(group) == 1)(swapped)
    pl.when(turns(group) == 1)(turned)


def neighbours(value):
    up, down = jnp.roll(value, -1, axis=0), jnp.roll(value, 1, axis=0)
    return jnp.where(iota(value.shape, 0) % 2 == 0, up, down)


def dealt(value, order):
    share = value.shape[0] // GROUP
    return jnp.concatenate([value[part * share : (part + 1) * share] for part in order], axis=0)


def pack_kernel(far_ref, u_ref, g_ref, y_ref, k_ref, out_ref, landed, rows, sems):
    chans = out_ref.shape[0] // ROLES
    copies = [
        pltpu.make_async_copy(ref, landed.at[role], sems.at[role])
        for role, ref in enumerate((u_ref, g_ref, y_ref, k_ref))
    ]
    for copy in copies:
        copy.start()
    for copy in copies:
        copy.wait()

    def store(order):
        for role in range(ROLES):
            rows[pl.ds(role, chans, stride=ROLES), :] = order(landed[role].astype(F32))
        out_ref[...] = rows[...].astype(BF16)

    by_group(far_ref[0], lambda: store(lambda value: value), lambda: store(neighbours), lambda: store(lambda value: dealt(value, HELD)))


def flip_rows(count, span):
    row, col = iota((count, count), 0), iota((count, count), 1)
    same = row // span == col // span
    return jnp.where(same & (row % span + col % span == span - 1), 1.0, 0.0).astype(BF16)


def take(rows, role, count):
    return rows[pl.ds(role, count, stride=ROLES), :]


def flipped_pair(gc, flip, lane_flip):
    high = gc.astype(BF16)
    low = (gc - high.astype(F32)).astype(BF16)
    both = jnp.concatenate([high, low], axis=0)
    both = jnp.dot(both, lane_flip, preferred_element_type=F32).astype(BF16)
    return jnp.dot(flip, both, preferred_element_type=F32)


def pad(padded, value, blocks):
    for part in range(padded.shape[0]):
        padded[part, :blocks, :] = jnp.zeros((blocks, LANES), F32)
        padded[part, blocks:, :] = value[part * blocks : (part + 1) * blocks]


def shifted(padded, d, blocks):
    parts = [padded[part, blocks - d : 2 * blocks - d, :] for part in range(padded.shape[0])]
    return jnp.concatenate(parts, axis=0).astype(BF16)


def skew(value):
    return pltpu.roll(value, 0, 1, stride=1, stride_axis=0)


def filt_kernel(blocks, in_ref, filt_ref, rows, padded):
    count = GROUP * blocks
    rows[...] = in_ref[...].astype(F32)
    u = take(rows, 0, count)
    gc = take(rows, 1, count) * take(rows, 2, count)
    high = gc.astype(BF16).astype(F32)
    low = gc - high
    for part in range(2 * GROUP):
        value = high if part < GROUP else low
        at = part % GROUP * blocks
        padded[part, :blocks, :] = value[at : at + blocks]
        padded[part, blocks:, :] = jnp.zeros((blocks, LANES), F32)
    left = lax.dot_general(
        flip_rows(LANES, LANES), u.astype(BF16), (((1,), (1,)), ((), ())), preferred_element_type=F32
    ).astype(BF16)
    left = jnp.concatenate([left, left], axis=1)
    wrapped = iota((LANES, LANES), 1) <= iota((LANES, LANES), 0)
    held = None
    for pair in range(blocks // 2):
        wide = []
        for d in (2 * pair, 2 * pair + 1):
            parts = [padded[part, d : d + blocks, :] for part in range(2 * GROUP)]
            wide.append(jnp.concatenate(parts, axis=0).astype(BF16))
        products = jnp.dot(left, jnp.concatenate(wide, axis=1), preferred_element_type=F32)
        for half in range(2):
            d = 2 * pair + half
            turned = pltpu.roll(products[:, half * LANES : (half + 1) * LANES], 1, 1, stride=1, stride_axis=0)
            if held is not None:
                filt_ref[d - 1 : d, :] = jnp.sum(jnp.where(wrapped, held, turned), axis=0, keepdims=True)
            held = turned
    filt_ref[blocks - 1 : blocks, :] = jnp.sum(jnp.where(wrapped, held, 0.0), axis=0, keepdims=True)


def convolve(blocks, chan_ref, gain_ref, in_ref, gate_ref, input_ref, rows, padded, gains, sem):
    count = GROUP * blocks
    fetch = pltpu.make_async_copy(gain_ref, gains, sem)
    fetch.start()
    rows[...] = in_ref[...].astype(F32)
    u = take(rows, 0, count)
    y = take(rows, 2, count)
    gc = take(rows, 1, count) * y
    k = take(rows, 3, blocks)
    lane_flip = flip_rows(LANES, LANES)
    flip = flip_rows(2 * count, blocks)
    both = flipped_pair(gc, flip, lane_flip)
    pad(padded, jnp.concatenate([u, both], axis=0), blocks)
    inside = iota((LANES, LANES), 1) >= iota((LANES, LANES), 0)
    before = jnp.zeros((LANES, LANES), F32)
    total = jnp.zeros((3 * count, LANES), F32)
    for pair in range(blocks // 2):
        signal, toeplitz = [], []
        for d in (2 * pair, 2 * pair + 1):
            signal.append(shifted(padded, d, blocks))
            rolled = skew(jnp.broadcast_to(k[d : d + 1, :], (LANES, LANES)))
            toeplitz.append(jnp.where(inside, rolled, before).astype(BF16))
            before = rolled
        total = total + jnp.dot(
            jnp.concatenate(signal, axis=1), jnp.concatenate(toeplitz, axis=0), preferred_element_type=F32
        )
    scale = 1.0 / 64.0
    fetch.wait()
    gain = gains[chan_ref[0]]
    gate_ref[...] = (y * (total[:count] * scale + gain * u)).astype(BF16)
    corr = total[count : 2 * count] + total[2 * count :]
    d_input = (corr * scale + gain * (both[:count] + both[count:])).astype(BF16)
    d_input = jnp.dot(d_input, lane_flip, preferred_element_type=F32).astype(BF16)
    input_ref[...] = jnp.dot(flip[:count, :count], d_input, preferred_element_type=F32).astype(BF16)


def early_kernel(blocks, far_ref, chan_ref, gain_ref, in_ref, filt_ref, gate_ref, input_ref, same_ref, *scratch):
    same_ref[...] = filt_ref[...]

    @pl.when(far_ref[0] == 0)
    def _():
        convolve(blocks, chan_ref, gain_ref, in_ref, gate_ref, input_ref, *scratch)


def late_kernel(
    blocks, far_ref, chan_ref, gain_ref, in_ref, early_gate_ref, early_input_ref, after_ref, gate_ref, input_ref, *scratch
):
    @pl.when(far_ref[0] == 0)
    def _():
        gate_ref[...] = early_gate_ref[...]
        input_ref[...] = early_input_ref[...]

    @pl.when(far_ref[0] != 0)
    def _():
        convolve(blocks, chan_ref, gain_ref, in_ref, gate_ref, input_ref, *scratch)


def add_kernel(left_ref, right_ref, out_ref):
    out_ref[...] = left_ref[...] + right_ref[...]


def last_kernel(pair_ref, own_ref, after_ref, out_ref):
    out_ref[...] = pair_ref[...] + own_ref[...]


def spread_kernel(blocks, far_ref, gate_ref, input_ref, *refs):
    *sums, out_ref, rows = refs
    count = GROUP * blocks
    group = far_ref[0]
    own, from_2, three, early, first, three_3, to_2 = [ref[...] for ref in sums]
    on_0, on_1, on_2, on_3 = three + from_2, early + first, to_2 + own, three_3 + early
    filt = jnp.where(group < 2, jnp.where(group == 0, on_0, on_1), jnp.where(group == 2, on_2, on_3))
    high = filt.astype(BF16).astype(F32)
    low = filt - high
    rows[pl.ds(0, count, stride=ROLES), :] = gate_ref[...].astype(F32)
    rows[pl.ds(1, count, stride=ROLES), :] = input_ref[...].astype(F32)
    for part in range(GROUP):
        at = part * blocks * ROLES
        rows[pl.ds(at + 2, blocks, stride=ROLES), :] = high
        rows[pl.ds(at + 3, blocks, stride=ROLES), :] = low
    out_ref[...] = rows[...].astype(BF16)


def unpack_kernel(far_ref, in_ref, input_ref, gate_ref, filt_ref, rows):
    chans = input_ref.shape[0]
    rows[...] = in_ref[...].astype(F32)

    def store(order):
        gate_ref[...] = order(take(rows, 0, chans)).astype(BF16)
        input_ref[...] = order(take(rows, 1, chans)).astype(BF16)
        filt_ref[...] = order(take(rows, 2, chans) + take(rows, 3, chans)) * (1.0 / 64.0)

    by_group(far_ref[0], lambda: store(lambda value: value), lambda: store(neighbours), lambda: store(lambda value: dealt(value, HOLDER)))


VMEM = pl.BlockSpec(memory_space=pltpu.VMEM)
SMEM = pl.BlockSpec(memory_space=pltpu.SMEM)


def shape(dims, dtype):
    return jax.ShapeDtypeStruct(dims, dtype)


HBM = pl.BlockSpec(memory_space=pltpu.HBM)


def in_hbm(array):
    return pltpu.with_memory_space_constraint(array, pltpu.HBM)


def call(kernel, outs, ins, scratch):
    return pl.pallas_call(
        kernel,
        out_shape=outs,
        in_specs=ins,
        out_specs=jax.tree.map(lambda _: VMEM, outs),
        scratch_shapes=scratch,
        compiler_params=pltpu.CompilerParams(vmem_limit_bytes=48 * 1024 * 1024),
    )


def send(array, *edges):
    near, seq = lax.axis_size("near"), lax.axis_size("seq")
    pairs = []
    for source, target in edges:
        crossed = swaps(source) ^ swaps(target)
        for i in range(near):
            share = HELD[i] if turns(source) else i
            to = HOLDER[share] if turns(target) else share
            pairs += [((source * near + i) * seq + j, (target * near + to) * seq + (j ^ crossed)) for j in range(seq)]
    return lax.ppermute(array, ("far", "near", "seq"), pairs)


def body(inputs, gate_values, grad_out, filter_raw, skip_gain):
    blocks = lax.axis_size("seq")
    far = lax.axis_index("far").reshape(1)
    chans = inputs.shape[1]
    count = GROUP * blocks
    rows = pltpu.VMEM((count * ROLES, LANES), F32)
    packed = call(
        pack_kernel,
        shape((chans * ROLES, LANES), BF16),
        [SMEM] + [HBM] * 4,
        [
            pltpu.VMEM((ROLES, chans, LANES), BF16),
            pltpu.VMEM((chans * ROLES, LANES), F32),
            pltpu.SemaphoreType.DMA((ROLES,)),
        ],
    )(far, *map(in_hbm, (inputs[0], gate_values[0], grad_out[0], filter_raw)))
    packed = lax.all_to_all(packed, ("near", "seq"), 0, 0, tiled=True)
    filt = call(
        lambda *refs: filt_kernel(blocks, *refs),
        shape((blocks, LANES), F32),
        [VMEM],
        [rows, pltpu.VMEM((2 * GROUP, 2 * blocks, LANES), F32)],
    )(packed)
    near = lax.axis_index("near")
    held = sum(jnp.where(near == i, share, 0) for i, share in enumerate(HELD))
    near = jnp.where(turns(far) == 1, held, near)
    chan = near * blocks + (lax.axis_index("seq") ^ swaps(far))
    out = shape((count, LANES), BF16)
    part = shape((blocks, LANES), F32)
    scratch = [
        rows,
        pltpu.VMEM((3 * GROUP, 2 * blocks, LANES), F32),
        pltpu.SMEM(skip_gain.shape, F32),
        pltpu.SemaphoreType.DMA(()),
    ]
    gain = in_hbm(skip_gain)
    gate, d_in, same = call(
        lambda *refs: early_kernel(blocks, *refs), (out, out, part), [SMEM, SMEM, HBM, VMEM, VMEM], scratch
    )(far, chan, gain, packed, filt)
    from_2 = send(filt, (2, 0))
    from_3 = send(filt, (3, 0))
    from_1 = send(filt, (1, 0))
    pair = call(add_kernel, part, [VMEM] * 2, [])(same, from_1)
    first = send(pair, (0, 3), (2, 1))
    three = call(add_kernel, part, [VMEM] * 2, [])(pair, from_3)
    early = send(three, (0, 1), (2, 3))
    three_3 = call(last_kernel, part, [VMEM] * 3, [])(first, same, from_2)
    to_2 = send(three_3, (3, 2))
    gate, d_in = call(
        lambda *refs: late_kernel(blocks, *refs), (out, out), [SMEM, SMEM, HBM] + [VMEM] * 4, scratch
    )(far, chan, gain, packed, gate, d_in, three)
    packed = call(
        lambda *refs: spread_kernel(blocks, *refs),
        shape((count * ROLES, LANES), BF16),
        [SMEM] + [VMEM] * 9,
        [rows],
    )(far, gate, d_in, same, from_2, three, early, first, three_3, to_2)
    packed = lax.all_to_all(packed, ("near", "seq"), 0, 0, tiled=True)
    d_input, d_gate, d_filter = call(
        unpack_kernel,
        (shape((chans, LANES), BF16), shape((chans, LANES), BF16), shape((chans, LANES), F32)),
        [SMEM, VMEM],
        [pltpu.VMEM((chans * ROLES, LANES), F32)],
    )(far, packed)
    return d_input[None], d_gate[None], d_filter


def solution(mesh):
    sizes = mesh.devices.shape
    mesh = Mesh(mesh.devices.reshape(sizes[0] // GROUP, GROUP, sizes[1]), ("far", "near", "seq"))
    signal = P(("far", "near"), None, "seq")
    return jax.shard_map(
        body,
        mesh=mesh,
        in_specs=(signal, signal, signal, P(None, "seq"), P()),
        out_specs=(signal, signal, P(None, "seq")),
        check_vma=False,
    )
```

```python
import jax
import jax.numpy as jnp
from jax import lax
from jax.experimental import pallas as pl
from jax.experimental.pallas import tpu as pltpu
from jax.sharding import Mesh, PartitionSpec as P

LANES = 128
GROUP = 4
ROLES = 4

F32 = jnp.float32
BF16 = jnp.bfloat16


def iota(shape, dim):
    return lax.broadcasted_iota(jnp.int32, shape, dim)


def swaps(group):
    return group % 2


HELD = (1, 0, 3, 2)
HOLDER = (1, 0, 3, 2)


def turns(group):
    return group // 2 * (1 - group % 2)


def by_group(group, plain, swapped, turned):
    pl.when(group == 0)(plain)
    pl.when(swaps(group) == 1)(swapped)
    pl.when(turns(group) == 1)(turned)


def neighbours(value):
    up, down = jnp.roll(value, -1, axis=0), jnp.roll(value, 1, axis=0)
    return jnp.where(iota(value.shape, 0) % 2 == 0, up, down)


def dealt(value, order):
    share = value.shape[0] // GROUP
    return jnp.concatenate([value[part * share : (part + 1) * share] for part in order], axis=0)


def pack_kernel(far_ref, u_ref, g_ref, y_ref, k_ref, out_ref, landed, rows, sems):
    chans = out_ref.shape[0] // ROLES
    copies = [
        pltpu.make_async_copy(ref, landed.at[role], sems.at[role])
        for role, ref in enumerate((u_ref, g_ref, y_ref, k_ref))
    ]
    for copy in copies:
        copy.start()
    for copy in copies:
        copy.wait()

    def store(order):
        for role in range(ROLES):
            rows[pl.ds(role, chans, stride=ROLES), :] = order(landed[role].astype(F32))
        out_ref[...] = rows[...].astype(BF16)

    by_group(far_ref[0], lambda: store(lambda value: value), lambda: store(neighbours), lambda: store(lambda value: dealt(value, HELD)))


def flip_rows(count, span):
    row, col = iota((count, count), 0), iota((count, count), 1)
    same = row // span == col // span
    return jnp.where(same & (row % span + col % span == span - 1), 1.0, 0.0).astype(BF16)


def take(rows, role, count):
    return rows[pl.ds(role, count, stride=ROLES), :]


def flipped_pair(gc, flip, lane_flip):
    high = gc.astype(BF16)
    low = (gc - high.astype(F32)).astype(BF16)
    both = jnp.concatenate([high, low], axis=0)
    both = jnp.dot(both, lane_flip, preferred_element_type=F32).astype(BF16)
    return jnp.dot(flip, both, preferred_element_type=F32)


def pad(padded, value, blocks):
    for part in range(padded.shape[0]):
        padded[part, :blocks, :] = jnp.zeros((blocks, LANES), F32)
        padded[part, blocks:, :] = value[part * blocks : (part + 1) * blocks]


def shifted(padded, d, blocks):
    parts = [padded[part, blocks - d : 2 * blocks - d, :] for part in range(padded.shape[0])]
    return jnp.concatenate(parts, axis=0).astype(BF16)


def skew(value):
    return pltpu.roll(value, 0, 1, stride=1, stride_axis=0)


def filt_kernel(blocks, in_ref, filt_ref, rows, padded):
    count = GROUP * blocks
    rows[...] = in_ref[...].astype(F32)
    u = take(rows, 0, count)
    gc = take(rows, 1, count) * take(rows, 2, count)
    high = gc.astype(BF16).astype(F32)
    low = gc - high
    for part in range(2 * GROUP):
        value = high if part < GROUP else low
        at = part % GROUP * blocks
        padded[part, :blocks, :] = value[at : at + blocks]
        padded[part, blocks:, :] = jnp.zeros((blocks, LANES), F32)
    left = lax.dot_general(
        flip_rows(LANES, LANES), u.astype(BF16), (((1,), (1,)), ((), ())), preferred_element_type=F32
    ).astype(BF16)
    left = jnp.concatenate([left, left], axis=1)
    wrapped = iota((LANES, LANES), 1) <= iota((LANES, LANES), 0)
    held = None
    for pair in range(blocks // 2):
        wide = []
        for d in (2 * pair, 2 * pair + 1):
            parts = [padded[part, d : d + blocks, :] for part in range(2 * GROUP)]
            wide.append(jnp.concatenate(parts, axis=0).astype(BF16))
        products = jnp.dot(left, jnp.concatenate(wide, axis=1), preferred_element_type=F32)
        for half in range(2):
            d = 2 * pair + half
            turned = pltpu.roll(products[:, half * LANES : (half + 1) * LANES], 1, 1, stride=1, stride_axis=0)
            if held is not None:
                filt_ref[d - 1 : d, :] = jnp.sum(jnp.where(wrapped, held, turned), axis=0, keepdims=True)
            held = turned
    filt_ref[blocks - 1 : blocks, :] = jnp.sum(jnp.where(wrapped, held, 0.0), axis=0, keepdims=True)


def convolve(blocks, chan_ref, gain_ref, in_ref, gate_ref, input_ref, rows, padded, gains, sem):
    count = GROUP * blocks
    fetch = pltpu.make_async_copy(gain_ref, gains, sem)
    fetch.start()
    rows[...] = in_ref[...].astype(F32)
    u = take(rows, 0, count)
    y = take(rows, 2, count)
    gc = take(rows, 1, count) * y
    k = take(rows, 3, blocks)
    lane_flip = flip_rows(LANES, LANES)
    flip = flip_rows(2 * count, blocks)
    both = flipped_pair(gc, flip, lane_flip)
    pad(padded, jnp.concatenate([u, both], axis=0), blocks)
    inside = iota((LANES, LANES), 1) >= iota((LANES, LANES), 0)
    before = jnp.zeros((LANES, LANES), F32)
    total = jnp.zeros((3 * count, LANES), F32)
    for pair in range(blocks // 2):
        signal, toeplitz = [], []
        for d in (2 * pair, 2 * pair + 1):
            signal.append(shifted(padded, d, blocks))
            rolled = skew(jnp.broadcast_to(k[d : d + 1, :], (LANES, LANES)))
            toeplitz.append(jnp.where(inside, rolled, before).astype(BF16))
            before = rolled
        total = total + jnp.dot(
            jnp.concatenate(signal, axis=1), jnp.concatenate(toeplitz, axis=0), preferred_element_type=F32
        )
    scale = 1.0 / 64.0
    fetch.wait()
    gain = gains[chan_ref[0]]
    gate_ref[...] = (y * (total[:count] * scale + gain * u)).astype(BF16)
    corr = total[count : 2 * count] + total[2 * count :]
    d_input = (corr * scale + gain * (both[:count] + both[count:])).astype(BF16)
    d_input = jnp.dot(d_input, lane_flip, preferred_element_type=F32).astype(BF16)
    input_ref[...] = jnp.dot(flip[:count, :count], d_input, preferred_element_type=F32).astype(BF16)


def early_kernel(blocks, far_ref, chan_ref, gain_ref, in_ref, filt_ref, gate_ref, input_ref, same_ref, *scratch):
    same_ref[...] = filt_ref[...]

    @pl.when(far_ref[0] == 0)
    def _():
        convolve(blocks, chan_ref, gain_ref, in_ref, gate_ref, input_ref, *scratch)


def late_kernel(
    blocks, far_ref, chan_ref, gain_ref, in_ref, early_gate_ref, early_input_ref, after_ref, gate_ref, input_ref, *scratch
):
    @pl.when(far_ref[0] == 0)
    def _():
        gate_ref[...] = early_gate_ref[...]
        input_ref[...] = early_input_ref[...]

    @pl.when(far_ref[0] != 0)
    def _():
        convolve(blocks, chan_ref, gain_ref, in_ref, gate_ref, input_ref, *scratch)


def add_kernel(left_ref, right_ref, out_ref):
    out_ref[...] = left_ref[...] + right_ref[...]


def last_kernel(pair_ref, own_ref, after_ref, out_ref):
    out_ref[...] = pair_ref[...] + own_ref[...]


def spread_kernel(blocks, far_ref, gate_ref, input_ref, *refs):
    *sums, out_ref, rows = refs
    count = GROUP * blocks
    group = far_ref[0]
    own, from_2, three, early, first, three_3, to_2 = [ref[...] for ref in sums]
    on_0, on_1, on_2, on_3 = three + from_2, early + first, to_2 + own, three_3 + early
    filt = jnp.where(group < 2, jnp.where(group == 0, on_0, on_1), jnp.where(group == 2, on_2, on_3))
    high = filt.astype(BF16).astype(F32)
    low = filt - high
    rows[pl.ds(0, count, stride=ROLES), :] = gate_ref[...].astype(F32)
    rows[pl.ds(1, count, stride=ROLES), :] = input_ref[...].astype(F32)
    for part in range(GROUP):
        at = part * blocks * ROLES
        rows[pl.ds(at + 2, blocks, stride=ROLES), :] = high
        rows[pl.ds(at + 3, blocks, stride=ROLES), :] = low
    out_ref[...] = rows[...].astype(BF16)


def unpack_kernel(far_ref, in_ref, input_ref, gate_ref, filt_ref, rows):
    chans = input_ref.shape[0]
    rows[...] = in_ref[...].astype(F32)

    def store(order):
        gate_ref[...] = order(take(rows, 0, chans)).astype(BF16)
        input_ref[...] = order(take(rows, 1, chans)).astype(BF16)
        filt_ref[...] = order(take(rows, 2, chans) + take(rows, 3, chans)) * (1.0 / 64.0)

    by_group(far_ref[0], lambda: store(lambda value: value), lambda: store(neighbours), lambda: store(lambda value: dealt(value, HOLDER)))


VMEM = pl.BlockSpec(memory_space=pltpu.VMEM)
SMEM = pl.BlockSpec(memory_space=pltpu.SMEM)


def shape(dims, dtype):
    return jax.ShapeDtypeStruct(dims, dtype)


HBM = pl.BlockSpec(memory_space=pltpu.HBM)


def in_hbm(array):
    return pltpu.with_memory_space_constraint(array, pltpu.HBM)


def call(kernel, outs, ins, scratch):
    return pl.pallas_call(
        kernel,
        out_shape=outs,
        in_specs=ins,
        out_specs=jax.tree.map(lambda _: VMEM, outs),
        scratch_shapes=scratch,
        compiler_params=pltpu.CompilerParams(vmem_limit_bytes=48 * 1024 * 1024),
    )


def send(array, *edges):
    near, seq = lax.axis_size("near"), lax.axis_size("seq")
    pairs = []
    for source, target in edges:
        crossed = swaps(source) ^ swaps(target)
        for i in range(near):
            share = HELD[i] if turns(source) else i
            to = HOLDER[share] if turns(target) else share
            pairs += [((source * near + i) * seq + j, (target * near + to) * seq + (j ^ crossed)) for j in range(seq)]
    return lax.ppermute(array, ("far", "near", "seq"), pairs)


def body(inputs, gate_values, grad_out, filter_raw, skip_gain):
    blocks = lax.axis_size("seq")
    far = lax.axis_index("far").reshape(1)
    chans = inputs.shape[1]
    count = GROUP * blocks
    rows = pltpu.VMEM((count * ROLES, LANES), F32)
    packed = call(
        pack_kernel,
        shape((chans * ROLES, LANES), BF16),
        [SMEM] + [HBM] * 4,
        [
            pltpu.VMEM((ROLES, chans, LANES), BF16),
            pltpu.VMEM((chans * ROLES, LANES), F32),
            pltpu.SemaphoreType.DMA((ROLES,)),
        ],
    )(far, *map(in_hbm, (inputs[0], gate_values[0], grad_out[0], filter_raw)))
    packed = lax.all_to_all(packed, ("near", "seq"), 0, 0, tiled=True)
    filt = call(
        lambda *refs: filt_kernel(blocks, *refs),
        shape((blocks, LANES), F32),
        [VMEM],
        [rows, pltpu.VMEM((2 * GROUP, 2 * blocks, LANES), F32)],
    )(packed)
    near = lax.axis_index("near")
    held = sum(jnp.where(near == i, share, 0) for i, share in enumerate(HELD))
    near = jnp.where(turns(far) == 1, held, near)
    chan = near * blocks + (lax.axis_index("seq") ^ swaps(far))
    out = shape((count, LANES), BF16)
    part = shape((blocks, LANES), F32)
    scratch = [
        rows,
        pltpu.VMEM((3 * GROUP, 2 * blocks, LANES), F32),
        pltpu.SMEM(skip_gain.shape, F32),
        pltpu.SemaphoreType.DMA(()),
    ]
    gain = in_hbm(skip_gain)
    gate, d_in, same = call(
        lambda *refs: early_kernel(blocks, *refs), (out, out, part), [SMEM, SMEM, HBM, VMEM, VMEM], scratch
    )(far, chan, gain, packed, filt)
    from_2 = send(filt, (2, 0))
    from_3 = send(filt, (3, 0))
    from_1 = send(filt, (1, 0))
    pair = call(add_kernel, part, [VMEM] * 2, [])(same, from_1)
    first = send(pair, (0, 3), (2, 1))
    three = call(add_kernel, part, [VMEM] * 2, [])(pair, from_3)
    early = send(three, (0, 1), (2, 3))
    three_3 = call(last_kernel, part, [VMEM] * 3, [])(first, same, from_2)
    to_2 = send(three_3, (3, 2))
    gate, d_in = call(
        lambda *refs: late_kernel(blocks, *refs), (out, out), [SMEM, SMEM, HBM] + [VMEM] * 4, scratch
    )(far, chan, gain, packed, gate, d_in, three)
    packed = call(
        lambda *refs: spread_kernel(blocks, *refs),
        shape((count * ROLES, LANES), BF16),
        [SMEM] + [VMEM] * 9,
        [rows],
    )(far, gate, d_in, same, from_2, three, early, first, three_3, to_2)
    packed = lax.all_to_all(packed, ("near", "seq"), 0, 0, tiled=True)
    d_input, d_gate, d_filter = call(
        unpack_kernel,
        (shape((chans, LANES), BF16), shape((chans, LANES), BF16), shape((chans, LANES), F32)),
        [SMEM, VMEM],
        [pltpu.VMEM((chans * ROLES, LANES), F32)],
    )(far, packed)
    return d_input[None], d_gate[None], d_filter


def solution(mesh):
    sizes = mesh.devices.shape
    mesh = Mesh(mesh.devices.reshape(sizes[0] // GROUP, GROUP, sizes[1]), ("far", "near", "seq"))
    signal = P(("far", "near"), None, "seq")
    return jax.shard_map(
        body,
        mesh=mesh,
        in_specs=(signal, signal, signal, P(None, "seq"), P()),
        out_specs=(signal, signal, P(None, "seq")),
        check_vma=False,
    )
```

```python
import jax
import jax.numpy as jnp
from jax import lax
from jax.experimental import pallas as pl
from jax.experimental.pallas import tpu as pltpu
from jax.sharding import Mesh, PartitionSpec as P

LANES = 128
GROUP = 4
ROLES = 4

F32 = jnp.float32
BF16 = jnp.bfloat16


def iota(shape, dim):
    return lax.broadcasted_iota(jnp.int32, shape, dim)


def swaps(group):
    return 1 - (group + 3) // 4


HELD = (1, 0, 3, 2)
HOLDER = (1, 0, 3, 2)


def turns(group):
    return group // 2 * (1 - group % 2)


def by_group(group, plain, swapped, turned):
    pl.when(group % 2 == 1)(plain)
    pl.when(swaps(group) == 1)(swapped)
    pl.when(turns(group) == 1)(turned)


def neighbours(value):
    up, down = jnp.roll(value, -1, axis=0), jnp.roll(value, 1, axis=0)
    return jnp.where(iota(value.shape, 0) % 2 == 0, up, down)


def dealt(value, order):
    share = value.shape[0] // GROUP
    return jnp.concatenate([value[part * share : (part + 1) * share] for part in order], axis=0)


def pack_kernel(far_ref, u_ref, g_ref, y_ref, k_ref, out_ref, landed, rows, sems):
    chans = out_ref.shape[0] // ROLES
    copies = [
        pltpu.make_async_copy(ref, landed.at[role], sems.at[role])
        for role, ref in enumerate((u_ref, g_ref, y_ref, k_ref))
    ]
    for copy in copies:
        copy.start()
    for copy in copies:
        copy.wait()

    def store(order):
        for role in range(ROLES):
            rows[pl.ds(role, chans, stride=ROLES), :] = order(landed[role].astype(F32))
        out_ref[...] = rows[...].astype(BF16)

    by_group(far_ref[0], lambda: store(lambda value: value), lambda: store(neighbours), lambda: store(lambda value: dealt(value, HELD)))


def flip_rows(count, span):
    row, col = iota((count, count), 0), iota((count, count), 1)
    same = row // span == col // span
    return jnp.where(same & (row % span + col % span == span - 1), 1.0, 0.0).astype(BF16)


def take(rows, role, count):
    return rows[pl.ds(role, count, stride=ROLES), :]


def flipped_pair(gc, flip, lane_flip):
    high = gc.astype(BF16)
    low = (gc - high.astype(F32)).astype(BF16)
    both = jnp.concatenate([high, low], axis=0)
    both = jnp.dot(both, lane_flip, preferred_element_type=F32).astype(BF16)
    return jnp.dot(flip, both, preferred_element_type=F32)


def pad(padded, value, blocks):
    for part in range(padded.shape[0]):
        padded[part, :blocks, :] = jnp.zeros((blocks, LANES), F32)
        padded[part, blocks:, :] = value[part * blocks : (part + 1) * blocks]


def shifted(padded, d, blocks):
    parts = [padded[part, blocks - d : 2 * blocks - d, :] for part in range(padded.shape[0])]
    return jnp.concatenate(parts, axis=0).astype(BF16)


def skew(value):
    return pltpu.roll(value, 0, 1, stride=1, stride_axis=0)


def filt_kernel(blocks, in_ref, filt_ref, rows, padded):
    count = GROUP * blocks
    rows[...] = in_ref[...].astype(F32)
    u = take(rows, 0, count)
    gc = take(rows, 1, count) * take(rows, 2, count)
    high = gc.astype(BF16).astype(F32)
    low = gc - high
    for part in range(2 * GROUP):
        value = high if part < GROUP else low
        at = part % GROUP * blocks
        padded[part, :blocks, :] = value[at : at + blocks]
        padded[part, blocks:, :] = jnp.zeros((blocks, LANES), F32)
    left = lax.dot_general(
        flip_rows(LANES, LANES), u.astype(BF16), (((1,), (1,)), ((), ())), preferred_element_type=F32
    ).astype(BF16)
    left = jnp.concatenate([left, left], axis=1)
    wrapped = iota((LANES, LANES), 1) <= iota((LANES, LANES), 0)
    held = None
    for pair in range(blocks // 2):
        wide = []
        for d in (2 * pair, 2 * pair + 1):
            parts = [padded[part, d : d + blocks, :] for part in range(2 * GROUP)]
            wide.append(jnp.concatenate(parts, axis=0).astype(BF16))
        products = jnp.dot(left, jnp.concatenate(wide, axis=1), preferred_element_type=F32)
        for half in range(2):
            d = 2 * pair + half
            turned = pltpu.roll(products[:, half * LANES : (half + 1) * LANES], 1, 1, stride=1, stride_axis=0)
            if held is not None:
                filt_ref[d - 1 : d, :] = jnp.sum(jnp.where(wrapped, held, turned), axis=0, keepdims=True)
            held = turned
    filt_ref[blocks - 1 : blocks, :] = jnp.sum(jnp.where(wrapped, held, 0.0), axis=0, keepdims=True)


def convolve(blocks, chan_ref, gain_ref, in_ref, gate_ref, input_ref, rows, padded, gains, sem):
    count = GROUP * blocks
    fetch = pltpu.make_async_copy(gain_ref, gains, sem)
    fetch.start()
    rows[...] = in_ref[...].astype(F32)
    u = take(rows, 0, count)
    y = take(rows, 2, count)
    gc = take(rows, 1, count) * y
    k = take(rows, 3, blocks)
    lane_flip = flip_rows(LANES, LANES)
    flip = flip_rows(2 * count, blocks)
    both = flipped_pair(gc, flip, lane_flip)
    pad(padded, jnp.concatenate([u, both], axis=0), blocks)
    inside = iota((LANES, LANES), 1) >= iota((LANES, LANES), 0)
    before = jnp.zeros((LANES, LANES), F32)
    total = jnp.zeros((3 * count, LANES), F32)
    for pair in range(blocks // 2):
        signal, toeplitz = [], []
        for d in (2 * pair, 2 * pair + 1):
            signal.append(shifted(padded, d, blocks))
            rolled = skew(jnp.broadcast_to(k[d : d + 1, :], (LANES, LANES)))
            toeplitz.append(jnp.where(inside, rolled, before).astype(BF16))
            before = rolled
        total = total + jnp.dot(
            jnp.concatenate(signal, axis=1), jnp.concatenate(toeplitz, axis=0), preferred_element_type=F32
        )
    scale = 1.0 / 64.0
    fetch.wait()
    gain = gains[chan_ref[0]]
    gate_ref[...] = (y * (total[:count] * scale + gain * u)).astype(BF16)
    corr = total[count : 2 * count] + total[2 * count :]
    d_input = (corr * scale + gain * (both[:count] + both[count:])).astype(BF16)
    d_input = jnp.dot(d_input, lane_flip, preferred_element_type=F32).astype(BF16)
    input_ref[...] = jnp.dot(flip[:count, :count], d_input, preferred_element_type=F32).astype(BF16)


def early_kernel(blocks, far_ref, chan_ref, gain_ref, in_ref, filt_ref, gate_ref, input_ref, same_ref, *scratch):
    same_ref[...] = filt_ref[...]

    @pl.when(far_ref[0] == 0)
    def _():
        convolve(blocks, chan_ref, gain_ref, in_ref, gate_ref, input_ref, *scratch)


def late_kernel(
    blocks, far_ref, chan_ref, gain_ref, in_ref, early_gate_ref, early_input_ref, after_ref, gate_ref, input_ref, *scratch
):
    @pl.when(far_ref[0] == 0)
    def _():
        gate_ref[...] = early_gate_ref[...]
        input_ref[...] = early_input_ref[...]

    @pl.when(far_ref[0] != 0)
    def _():
        convolve(blocks, chan_ref, gain_ref, in_ref, gate_ref, input_ref, *scratch)


def add_kernel(left_ref, right_ref, out_ref):
    out_ref[...] = left_ref[...] + right_ref[...]


def last_kernel(pair_ref, own_ref, after_ref, out_ref):
    out_ref[...] = pair_ref[...] + own_ref[...]


def spread_kernel(blocks, far_ref, gate_ref, input_ref, *refs):
    *sums, out_ref, rows = refs
    count = GROUP * blocks
    group = far_ref[0]
    own, from_2, three, early, first, three_3, to_2 = [ref[...] for ref in sums]
    on_0, on_1, on_2, on_3 = three + from_2, early + first, to_2 + own, three_3 + early
    filt = jnp.where(group < 2, jnp.where(group == 0, on_0, on_1), jnp.where(group == 2, on_2, on_3))
    high = filt.astype(BF16).astype(F32)
    low = filt - high
    rows[pl.ds(0, count, stride=ROLES), :] = gate_ref[...].astype(F32)
    rows[pl.ds(1, count, stride=ROLES), :] = input_ref[...].astype(F32)
    for part in range(GROUP):
        at = part * blocks * ROLES
        rows[pl.ds(at + 2, blocks, stride=ROLES), :] = high
        rows[pl.ds(at + 3, blocks, stride=ROLES), :] = low
    out_ref[...] = rows[...].astype(BF16)


def unpack_kernel(far_ref, in_ref, input_ref, gate_ref, filt_ref, rows):
    chans = input_ref.shape[0]
    rows[...] = in_ref[...].astype(F32)

    def store(order):
        gate_ref[...] = order(take(rows, 0, chans)).astype(BF16)
        input_ref[...] = order(take(rows, 1, chans)).astype(BF16)
        filt_ref[...] = order(take(rows, 2, chans) + take(rows, 3, chans)) * (1.0 / 64.0)

    by_group(far_ref[0], lambda: store(lambda value: value), lambda: store(neighbours), lambda: store(lambda value: dealt(value, HOLDER)))


VMEM = pl.BlockSpec(memory_space=pltpu.VMEM)
SMEM = pl.BlockSpec(memory_space=pltpu.SMEM)


def shape(dims, dtype):
    return jax.ShapeDtypeStruct(dims, dtype)


HBM = pl.BlockSpec(memory_space=pltpu.HBM)


def in_hbm(array):
    return pltpu.with_memory_space_constraint(array, pltpu.HBM)


def call(kernel, outs, ins, scratch):
    return pl.pallas_call(
        kernel,
        out_shape=outs,
        in_specs=ins,
        out_specs=jax.tree.map(lambda _: VMEM, outs),
        scratch_shapes=scratch,
        compiler_params=pltpu.CompilerParams(vmem_limit_bytes=48 * 1024 * 1024),
    )


def send(array, *edges):
    near, seq = lax.axis_size("near"), lax.axis_size("seq")
    pairs = []
    for source, target in edges:
        crossed = swaps(source) ^ swaps(target)
        for i in range(near):
            share = HELD[i] if turns(source) else i
            to = HOLDER[share] if turns(target) else share
            pairs += [((source * near + i) * seq + j, (target * near + to) * seq + (j ^ crossed)) for j in range(seq)]
    return lax.ppermute(array, ("far", "near", "seq"), pairs)


def body(inputs, gate_values, grad_out, filter_raw, skip_gain):
    blocks = lax.axis_size("seq")
    far = lax.axis_index("far").reshape(1)
    chans = inputs.shape[1]
    count = GROUP * blocks
    rows = pltpu.VMEM((count * ROLES, LANES), F32)
    packed = call(
        pack_kernel,
        shape((chans * ROLES, LANES), BF16),
        [SMEM] + [HBM] * 4,
        [
            pltpu.VMEM((ROLES, chans, LANES), BF16),
            pltpu.VMEM((chans * ROLES, LANES), F32),
            pltpu.SemaphoreType.DMA((ROLES,)),
        ],
    )(far, *map(in_hbm, (inputs[0], gate_values[0], grad_out[0], filter_raw)))
    packed = lax.all_to_all(packed, ("near", "seq"), 0, 0, tiled=True)
    filt = call(
        lambda *refs: filt_kernel(blocks, *refs),
        shape((blocks, LANES), F32),
        [VMEM],
        [rows, pltpu.VMEM((2 * GROUP, 2 * blocks, LANES), F32)],
    )(packed)
    near = lax.axis_index("near")
    held = sum(jnp.where(near == i, share, 0) for i, share in enumerate(HELD))
    near = jnp.where(turns(far) == 1, held, near)
    chan = near * blocks + (lax.axis_index("seq") ^ swaps(far))
    out = shape((count, LANES), BF16)
    part = shape((blocks, LANES), F32)
    scratch = [
        rows,
        pltpu.VMEM((3 * GROUP, 2 * blocks, LANES), F32),
        pltpu.SMEM(skip_gain.shape, F32),
        pltpu.SemaphoreType.DMA(()),
    ]
    gain = in_hbm(skip_gain)
    gate, d_in, same = call(
        lambda *refs: early_kernel(blocks, *refs), (out, out, part), [SMEM, SMEM, HBM, VMEM, VMEM], scratch
    )(far, chan, gain, packed, filt)
    from_2 = send(filt, (2, 0))
    from_3 = send(filt, (3, 0))
    from_1 = send(filt, (1, 0))
    pair = call(add_kernel, part, [VMEM] * 2, [])(same, from_1)
    first = send(pair, (0, 3), (2, 1))
    three = call(add_kernel, part, [VMEM] * 2, [])(pair, from_3)
    early = send(three, (0, 1), (2, 3))
    three_3 = call(last_kernel, part, [VMEM] * 3, [])(first, same, from_2)
    to_2 = send(three_3, (3, 2))
    gate, d_in = call(
        lambda *refs: late_kernel(blocks, *refs), (out, out), [SMEM, SMEM, HBM] + [VMEM] * 4, scratch
    )(far, chan, gain, packed, gate, d_in, three)
    packed = call(
        lambda *refs: spread_kernel(blocks, *refs),
        shape((count * ROLES, LANES), BF16),
        [SMEM] + [VMEM] * 9,
        [rows],
    )(far, gate, d_in, same, from_2, three, early, first, three_3, to_2)
    packed = lax.all_to_all(packed, ("near", "seq"), 0, 0, tiled=True)
    d_input, d_gate, d_filter = call(
        unpack_kernel,
        (shape((chans, LANES), BF16), shape((chans, LANES), BF16), shape((chans, LANES), F32)),
        [SMEM, VMEM],
        [pltpu.VMEM((chans * ROLES, LANES), F32)],
    )(far, packed)
    return d_input[None], d_gate[None], d_filter


def solution(mesh):
    sizes = mesh.devices.shape
    mesh = Mesh(mesh.devices.reshape(sizes[0] // GROUP, GROUP, sizes[1]), ("far", "near", "seq"))
    signal = P(("far", "near"), None, "seq")
    return jax.shard_map(
        body,
        mesh=mesh,
        in_specs=(signal, signal, signal, P(None, "seq"), P()),
        out_specs=(signal, signal, P(None, "seq")),
        check_vma=False,
    )
```

```python
import jax
import jax.numpy as jnp
from jax import lax
from jax.experimental import pallas as pl
from jax.experimental.pallas import tpu as pltpu
from jax.sharding import Mesh, PartitionSpec as P

LANES = 128
GROUP = 4
ROLES = 4

F32 = jnp.float32
BF16 = jnp.bfloat16


def iota(shape, dim):
    return lax.broadcasted_iota(jnp.int32, shape, dim)


def swaps(group):
    return group // 3


HELD = (1, 0, 3, 2)
HOLDER = (1, 0, 3, 2)


def turns(group):
    return group // 2 * (1 - group % 2)


def by_group(group, plain, swapped, turned):
    pl.when(group < 2)(plain)
    pl.when(swaps(group) == 1)(swapped)
    pl.when(turns(group) == 1)(turned)


def neighbours(value):
    up, down = jnp.roll(value, -1, axis=0), jnp.roll(value, 1, axis=0)
    return jnp.where(iota(value.shape, 0) % 2 == 0, up, down)


def dealt(value, order):
    share = value.shape[0] // GROUP
    return jnp.concatenate([value[part * share : (part + 1) * share] for part in order], axis=0)


def pack_kernel(far_ref, u_ref, g_ref, y_ref, k_ref, out_ref, landed, rows, sems):
    chans = out_ref.shape[0] // ROLES
    copies = [
        pltpu.make_async_copy(ref, landed.at[role], sems.at[role])
        for role, ref in enumerate((u_ref, g_ref, y_ref, k_ref))
    ]
    for copy in copies:
        copy.start()
    for copy in copies:
        copy.wait()

    def store(order):
        for role in range(ROLES):
            rows[pl.ds(role, chans, stride=ROLES), :] = order(landed[role].astype(F32))
        out_ref[...] = rows[...].astype(BF16)

    by_group(far_ref[0], lambda: store(lambda value: value), lambda: store(neighbours), lambda: store(lambda value: dealt(value, HELD)))


def flip_rows(count, span):
    row, col = iota((count, count), 0), iota((count, count), 1)
    same = row // span == col // span
    return jnp.where(same & (row % span + col % span == span - 1), 1.0, 0.0).astype(BF16)


def take(rows, role, count):
    return rows[pl.ds(role, count, stride=ROLES), :]


def flipped_pair(gc, flip, lane_flip):
    high = gc.astype(BF16)
    low = (gc - high.astype(F32)).astype(BF16)
    both = jnp.concatenate([high, low], axis=0)
    both = jnp.dot(both, lane_flip, preferred_element_type=F32).astype(BF16)
    return jnp.dot(flip, both, preferred_element_type=F32)


def pad(padded, value, blocks):
    for part in range(padded.shape[0]):
        padded[part, :blocks, :] = jnp.zeros((blocks, LANES), F32)
        padded[part, blocks:, :] = value[part * blocks : (part + 1) * blocks]


def shifted(padded, d, blocks):
    parts = [padded[part, blocks - d : 2 * blocks - d, :] for part in range(padded.shape[0])]
    return jnp.concatenate(parts, axis=0).astype(BF16)


def skew(value):
    return pltpu.roll(value, 0, 1, stride=1, stride_axis=0)


def filt_kernel(blocks, in_ref, filt_ref, rows, padded):
    count = GROUP * blocks
    rows[...] = in_ref[...].astype(F32)
    u = take(rows, 0, count)
    gc = take(rows, 1, count) * take(rows, 2, count)
    high = gc.astype(BF16).astype(F32)
    low = gc - high
    for part in range(2 * GROUP):
        value = high if part < GROUP else low
        at = part % GROUP * blocks
        padded[part, :blocks, :] = value[at : at + blocks]
        padded[part, blocks:, :] = jnp.zeros((blocks, LANES), F32)
    left = lax.dot_general(
        flip_rows(LANES, LANES), u.astype(BF16), (((1,), (1,)), ((), ())), preferred_element_type=F32
    ).astype(BF16)
    left = jnp.concatenate([left, left], axis=1)
    wrapped = iota((LANES, LANES), 1) <= iota((LANES, LANES), 0)
    held = None
    for pair in range(blocks // 2):
        wide = []
        for d in (2 * pair, 2 * pair + 1):
            parts = [padded[part, d : d + blocks, :] for part in range(2 * GROUP)]
            wide.append(jnp.concatenate(parts, axis=0).astype(BF16))
        products = jnp.dot(left, jnp.concatenate(wide, axis=1), preferred_element_type=F32)
        for half in range(2):
            d = 2 * pair + half
            turned = pltpu.roll(products[:, half * LANES : (half + 1) * LANES], 1, 1, stride=1, stride_axis=0)
            if held is not None:
                filt_ref[d - 1 : d, :] = jnp.sum(jnp.where(wrapped, held, turned), axis=0, keepdims=True)
            held = turned
    filt_ref[blocks - 1 : blocks, :] = jnp.sum(jnp.where(wrapped, held, 0.0), axis=0, keepdims=True)


def convolve(blocks, chan_ref, gain_ref, in_ref, gate_ref, input_ref, rows, padded, gains, sem):
    count = GROUP * blocks
    fetch = pltpu.make_async_copy(gain_ref, gains, sem)
    fetch.start()
    rows[...] = in_ref[...].astype(F32)
    u = take(rows, 0, count)
    y = take(rows, 2, count)
    gc = take(rows, 1, count) * y
    k = take(rows, 3, blocks)
    lane_flip = flip_rows(LANES, LANES)
    flip = flip_rows(2 * count, blocks)
    both = flipped_pair(gc, flip, lane_flip)
    pad(padded, jnp.concatenate([u, both], axis=0), blocks)
    inside = iota((LANES, LANES), 1) >= iota((LANES, LANES), 0)
    before = jnp.zeros((LANES, LANES), F32)
    total = jnp.zeros((3 * count, LANES), F32)
    for pair in range(blocks // 2):
        signal, toeplitz = [], []
        for d in (2 * pair, 2 * pair + 1):
            signal.append(shifted(padded, d, blocks))
            rolled = skew(jnp.broadcast_to(k[d : d + 1, :], (LANES, LANES)))
            toeplitz.append(jnp.where(inside, rolled, before).astype(BF16))
            before = rolled
        total = total + jnp.dot(
            jnp.concatenate(signal, axis=1), jnp.concatenate(toeplitz, axis=0), preferred_element_type=F32
        )
    scale = 1.0 / 64.0
    fetch.wait()
    gain = gains[chan_ref[0]]
    gate_ref[...] = (y * (total[:count] * scale + gain * u)).astype(BF16)
    corr = total[count : 2 * count] + total[2 * count :]
    d_input = (corr * scale + gain * (both[:count] + both[count:])).astype(BF16)
    d_input = jnp.dot(d_input, lane_flip, preferred_element_type=F32).astype(BF16)
    input_ref[...] = jnp.dot(flip[:count, :count], d_input, preferred_element_type=F32).astype(BF16)


def early_kernel(blocks, far_ref, chan_ref, gain_ref, in_ref, filt_ref, gate_ref, input_ref, same_ref, *scratch):
    same_ref[...] = filt_ref[...]

    @pl.when(far_ref[0] == 0)
    def _():
        convolve(blocks, chan_ref, gain_ref, in_ref, gate_ref, input_ref, *scratch)


def late_kernel(
    blocks, far_ref, chan_ref, gain_ref, in_ref, early_gate_ref, early_input_ref, after_ref, gate_ref, input_ref, *scratch
):
    @pl.when(far_ref[0] == 0)
    def _():
        gate_ref[...] = early_gate_ref[...]
        input_ref[...] = early_input_ref[...]

    @pl.when(far_ref[0] != 0)
    def _():
        convolve(blocks, chan_ref, gain_ref, in_ref, gate_ref, input_ref, *scratch)


def add_kernel(left_ref, right_ref, out_ref):
    out_ref[...] = left_ref[...] + right_ref[...]


def last_kernel(pair_ref, own_ref, after_ref, out_ref):
    out_ref[...] = pair_ref[...] + own_ref[...]


def spread_kernel(blocks, far_ref, gate_ref, input_ref, *refs):
    *sums, out_ref, rows = refs
    count = GROUP * blocks
    group = far_ref[0]
    own, from_2, three, early, first, three_3, to_2 = [ref[...] for ref in sums]
    on_0, on_1, on_2, on_3 = three + from_2, early + first, to_2 + own, three_3 + early
    filt = jnp.where(group < 2, jnp.where(group == 0, on_0, on_1), jnp.where(group == 2, on_2, on_3))
    high = filt.astype(BF16).astype(F32)
    low = filt - high
    rows[pl.ds(0, count, stride=ROLES), :] = gate_ref[...].astype(F32)
    rows[pl.ds(1, count, stride=ROLES), :] = input_ref[...].astype(F32)
    for part in range(GROUP):
        at = part * blocks * ROLES
        rows[pl.ds(at + 2, blocks, stride=ROLES), :] = high
        rows[pl.ds(at + 3, blocks, stride=ROLES), :] = low
    out_ref[...] = rows[...].astype(BF16)


def unpack_kernel(far_ref, in_ref, input_ref, gate_ref, filt_ref, rows):
    chans = input_ref.shape[0]
    rows[...] = in_ref[...].astype(F32)

    def store(order):
        gate_ref[...] = order(take(rows, 0, chans)).astype(BF16)
        input_ref[...] = order(take(rows, 1, chans)).astype(BF16)
        filt_ref[...] = order(take(rows, 2, chans) + take(rows, 3, chans)) * (1.0 / 64.0)

    by_group(far_ref[0], lambda: store(lambda value: value), lambda: store(neighbours), lambda: store(lambda value: dealt(value, HOLDER)))


VMEM = pl.BlockSpec(memory_space=pltpu.VMEM)
SMEM = pl.BlockSpec(memory_space=pltpu.SMEM)


def shape(dims, dtype):
    return jax.ShapeDtypeStruct(dims, dtype)


HBM = pl.BlockSpec(memory_space=pltpu.HBM)


def in_hbm(array):
    return pltpu.with_memory_space_constraint(array, pltpu.HBM)


def call(kernel, outs, ins, scratch):
    return pl.pallas_call(
        kernel,
        out_shape=outs,
        in_specs=ins,
        out_specs=jax.tree.map(lambda _: VMEM, outs),
        scratch_shapes=scratch,
        compiler_params=pltpu.CompilerParams(vmem_limit_bytes=48 * 1024 * 1024),
    )


def send(array, *edges):
    near, seq = lax.axis_size("near"), lax.axis_size("seq")
    pairs = []
    for source, target in edges:
        crossed = swaps(source) ^ swaps(target)
        for i in range(near):
            share = HELD[i] if turns(source) else i
            to = HOLDER[share] if turns(target) else share
            pairs += [((source * near + i) * seq + j, (target * near + to) * seq + (j ^ crossed)) for j in range(seq)]
    return lax.ppermute(array, ("far", "near", "seq"), pairs)


def body(inputs, gate_values, grad_out, filter_raw, skip_gain):
    blocks = lax.axis_size("seq")
    far = lax.axis_index("far").reshape(1)
    chans = inputs.shape[1]
    count = GROUP * blocks
    rows = pltpu.VMEM((count * ROLES, LANES), F32)
    packed = call(
        pack_kernel,
        shape((chans * ROLES, LANES), BF16),
        [SMEM] + [HBM] * 4,
        [
            pltpu.VMEM((ROLES, chans, LANES), BF16),
            pltpu.VMEM((chans * ROLES, LANES), F32),
            pltpu.SemaphoreType.DMA((ROLES,)),
        ],
    )(far, *map(in_hbm, (inputs[0], gate_values[0], grad_out[0], filter_raw)))
    packed = lax.all_to_all(packed, ("near", "seq"), 0, 0, tiled=True)
    filt = call(
        lambda *refs: filt_kernel(blocks, *refs),
        shape((blocks, LANES), F32),
        [VMEM],
        [rows, pltpu.VMEM((2 * GROUP, 2 * blocks, LANES), F32)],
    )(packed)
    near = lax.axis_index("near")
    held = sum(jnp.where(near == i, share, 0) for i, share in enumerate(HELD))
    near = jnp.where(turns(far) == 1, held, near)
    chan = near * blocks + (lax.axis_index("seq") ^ swaps(far))
    out = shape((count, LANES), BF16)
    part = shape((blocks, LANES), F32)
    scratch = [
        rows,
        pltpu.VMEM((3 * GROUP, 2 * blocks, LANES), F32),
        pltpu.SMEM(skip_gain.shape, F32),
        pltpu.SemaphoreType.DMA(()),
    ]
    gain = in_hbm(skip_gain)
    gate, d_in, same = call(
        lambda *refs: early_kernel(blocks, *refs), (out, out, part), [SMEM, SMEM, HBM, VMEM, VMEM], scratch
    )(far, chan, gain, packed, filt)
    from_2 = send(filt, (2, 0))
    from_3 = send(filt, (3, 0))
    from_1 = send(filt, (1, 0))
    pair = call(add_kernel, part, [VMEM] * 2, [])(same, from_1)
    first = send(pair, (0, 3), (2, 1))
    three = call(add_kernel, part, [VMEM] * 2, [])(pair, from_3)
    early = send(three, (0, 1), (2, 3))
    three_3 = call(last_kernel, part, [VMEM] * 3, [])(first, same, from_2)
    to_2 = send(three_3, (3, 2))
    gate, d_in = call(
        lambda *refs: late_kernel(blocks, *refs), (out, out), [SMEM, SMEM, HBM] + [VMEM] * 4, scratch
    )(far, chan, gain, packed, gate, d_in, three)
    packed = call(
        lambda *refs: spread_kernel(blocks, *refs),
        shape((count * ROLES, LANES), BF16),
        [SMEM] + [VMEM] * 9,
        [rows],
    )(far, gate, d_in, same, from_2, three, early, first, three_3, to_2)
    packed = lax.all_to_all(packed, ("near", "seq"), 0, 0, tiled=True)
    d_input, d_gate, d_filter = call(
        unpack_kernel,
        (shape((chans, LANES), BF16), shape((chans, LANES), BF16), shape((chans, LANES), F32)),
        [SMEM, VMEM],
        [pltpu.VMEM((chans * ROLES, LANES), F32)],
    )(far, packed)
    return d_input[None], d_gate[None], d_filter


def solution(mesh):
    sizes = mesh.devices.shape
    mesh = Mesh(mesh.devices.reshape(sizes[0] // GROUP, GROUP, sizes[1]), ("far", "near", "seq"))
    signal = P(("far", "near"), None, "seq")
    return jax.shard_map(
        body,
        mesh=mesh,
        in_specs=(signal, signal, signal, P(None, "seq"), P()),
        out_specs=(signal, signal, P(None, "seq")),
        check_vma=False,
    )
```
